32 devices in a mesh: section: 2 (over core), seq: 16 (over z, y, x).
Axes of the slice: x: 2, y: 2, z: 4, core: 2. Of those that a mesh axis runs over, the one named last changes fastest.
Arguments:
- inputs: bfloat16 [8, 2048, 1024], P(None, 'seq'), may hold values from -6 to 6
- cotangent: bfloat16 [8, 2048, 1024], P(None, 'seq'), may hold values from -6 to 6
- lengths: int32 [8, 2], replicated, may hold values from 0 to 2048, as said below
- keep: float32 [8, 2048], P(None, 'seq'), may hold values from 0.0625 to 1
- init_states: float32 [2, 8, 512], P('section'), may hold values from -6 to 6
- ln_gain: float32 [2, 1024], P('section'), may hold values from 0.5 to 1.5
- ln_bias: float32 [2, 1024], P('section'), may hold values from -1.5 to 1.5
- w_gate: bfloat16 [2, 1024, 3072], P('section'), may hold values from -0.1875 to 0.1875
- w_value: bfloat16 [2, 1024, 512], P('section'), may hold values from -0.1875 to 0.1875
- in_map: bfloat16 [2, 512, 512], P('section'), may hold values from -0.25 to 0.25
- rates: float32 [2, 512], P('section'), may hold values from 4.8828125e-05 to 0.0333333333
- out_map: bfloat16 [2, 512, 512], P('section'), may hold values from -0.5 to 0.5
- w_mix: bfloat16 [2, 512, 3072], P('section'), may hold values from -0.25 to 0.25
- w_down: bfloat16 [2, 3072, 1024], P('section'), may hold values from -0.3125 to 0.3125
Outputs:
- block_out: bfloat16 [2, 8, 2048, 1024], P('section', None, 'seq')
- grad_in: float32 [2, 8, 2048, 1024], P('section', None, 'seq')
- piece_ends: float32 [2, 8, 16, 512], P('section', None, 'seq')
- grad_ln_gain: float32 [2, 1024], P('section', 'seq')
- grad_ln_bias: float32 [2, 1024], P('section', 'seq')
- grad_w_gate: float32 [2, 1024, 3072], P('section', 'seq')
- grad_w_value: float32 [2, 1024, 512], P('section', 'seq')
- grad_in_map: float32 [2, 512, 512], P('section', 'seq')
- grad_rates: float32 [2, 512], P('section', 'seq')
- grad_out_map: float32 [2, 512, 512], P('section', 'seq')
- grad_w_mix: float32 [2, 512, 3072], P('section', 'seq')
- grad_w_down: float32 [2, 3072, 1024], P('section', 'seq')
The draws below stay inside these ranges and needn't reach their ends.
Inputs may be any that keep to these rules, and one draw needn't show every extreme that they name: Row m holds a document of lengths[m, 0] positions from position 0, then one of lengths[m, 1] positions, then padding; a zero means no second document; every nonzero length is 1024 or more; in every draw some row holds a single document of 2048 positions.
All inputs are finite; a program needn't handle non-finite values.
Results may differ from the reference program's by a relative error of at most 0.02.
Values may be sent and summed in bfloat16 or wider, within the bound.
No kernel may reach another device: no remote copies, remote signals or barrier semaphores. Data moves between devices by JAX's collectives and lax.ppermute only.
A program may use at most 384 MiB of HBM per device.

```python
import jax
import jax.numpy as jnp
from jax import lax

D = 1024
FF = 3072
E = 512
NS = 512
MICRO = 8
TOK_DEV = 128
SHORTEST = 1024
ROW = 2048
N_SECTION = 2


def draw_lengths(key, part):
    key = jax.random.fold_in(key, 1)
    first_key, second_key, third_key = jax.random.split(key, 3)
    first_len = jax.random.randint(first_key, (MICRO,), SHORTEST, ROW - SHORTEST + 1)
    second_len = jax.random.randint(second_key, (MICRO,), SHORTEST, ROW - first_len + 1)
    full_row = jax.random.randint(third_key, (), 0, MICRO)
    chosen = jnp.arange(MICRO) == full_row
    first_len = jnp.where(chosen, ROW, first_len)
    second_len = jnp.where(chosen, 0, second_len)
    return jnp.stack([first_len, second_len], axis=-1).astype(jnp.int32)


def draw_keep(key, part):
    key = jax.random.fold_in(key, 2)
    first_key, second_key = jax.random.split(key)
    places = jax.random.randint(first_key, (MICRO, 4), 0, ROW)
    strength = jax.random.uniform(second_key, (MICRO, 4), jnp.float32, 0.5, 0.8)
    grid = jnp.arange(ROW)
    hits = grid[None, None, :] == places[:, :, None]
    return jnp.prod(jnp.where(hits, strength[:, :, None], 1.0), axis=1).astype(jnp.float32)


def draw_rates(key, part):
    key = jax.random.fold_in(key, 3)
    first_key, second_key, third_key = jax.random.split(key, 3)
    slow_share = 0.5
    chooser = jax.random.uniform(first_key, (N_SECTION, NS), jnp.float32)
    slow_rate = jnp.exp(jax.random.uniform(second_key, (N_SECTION, NS), jnp.float32, jnp.log(0.1 / ROW), jnp.log(1.0 / ROW)))
    fast_rate = jnp.exp(jax.random.uniform(third_key, (N_SECTION, NS), jnp.float32, jnp.log(1.0 / ROW), jnp.log(1.0 / 30.0)))
    return jnp.where(chooser < slow_share, slow_rate, fast_rate).astype(jnp.float32)


def steps_of(own_key, dims, cuts, low, top_value):
    loudness = 1.0
    for dim, blocks in cuts:
        steps = jax.random.uniform(jax.random.fold_in(jax.random.fold_in(own_key, 6), dim), (blocks,), jnp.float32, low / len(cuts), top_value / len(cuts))
        loudness = loudness * jnp.repeat(jnp.exp(steps), dims[dim] // blocks).reshape((-1,) + (1,) * (len(dims) - 1 - dim))
    return loudness


def normal_values(own_key, shape, deviation, reach, cuts=(), kind=jnp.bfloat16):
    entries = deviation * jax.random.normal(own_key, shape, jnp.float32)
    if cuts:
        entries = entries * steps_of(own_key, shape, cuts, -0.22, 0.18)
    return jnp.clip(entries, -reach, reach).astype(kind)


def setup_inputs(seed: int = 0) -> dict:
    splits = jax.random.split(jax.random.key(seed), 15)
    inputs = normal_values(splits[0], (MICRO, ROW, D), 1.0, 6.0, ((1, 16),))
    cotangent = normal_values(splits[1], (MICRO, ROW, D), 1.0, 6.0, ((1, 16),))
    lengths = draw_lengths(jax.random.fold_in(splits[14], 71), 0)
    keep = draw_keep(jax.random.fold_in(splits[14], 71), 0)
    init_states = normal_values(splits[4], (N_SECTION, MICRO, NS), 1.0, 6.0, ((0, 2),), jnp.float32)
    ln_gain = jnp.clip(1.0 + 0.1 * jax.random.normal(splits[5], (N_SECTION, D), jnp.float32), 0.5, 1.5)
    ln_bias = normal_values(splits[6], (N_SECTION, D), 0.3, 1.5, ((0, 2),), jnp.float32)
    w_gate = normal_values(splits[7], (N_SECTION, D, FF), D ** -0.5, 0.1875, ((0, 2),))
    w_value = normal_values(splits[8], (N_SECTION, D, E), D ** -0.5, 0.1875, ((0, 2),))
    in_map = normal_values(splits[9], (N_SECTION, E, NS), E ** -0.5, 0.25, ((0, 2),))
    rates = draw_rates(jax.random.fold_in(splits[14], 71), 0)
    out_map = normal_values(splits[11], (N_SECTION, NS, E), (NS // 4) ** -0.5, 0.5, ((0, 2),))
    w_mix = normal_values(splits[12], (N_SECTION, E, FF), E ** -0.5, 0.25, ((0, 2),))
    w_down = normal_values(splits[13], (N_SECTION, FF, D), (FF // 8) ** -0.5, 0.3125, ((0, 2),))
    return {"inputs": inputs, "cotangent": cotangent, "lengths": lengths, "keep": keep, "init_states": init_states, "ln_gain": ln_gain, "ln_bias": ln_bias, "w_gate": w_gate, "w_value": w_value, "in_map": in_map, "rates": rates, "out_map": out_map, "w_mix": w_mix, "w_down": w_down}


@jax.custom_vjp
def low(v):
    return lax.optimization_barrier(v.astype(jnp.bfloat16)).astype(jnp.float32)

@jax.custom_vjp
def low_back(v):
    return v

def low_keep(v):
    return (low(v), None)

def low_pass(kept, grad):
    return (grad,)

def back_keep(v):
    return (v, None)

def back_low(kept, grad):
    return (low(grad),)
low.defvjp(low_keep, low_pass)
low_back.defvjp(back_keep, back_low)

def matmul(left, right):
    return jnp.dot(left, right, precision=lax.Precision.HIGHEST, preferred_element_type=jnp.float32)

def chain_step(earlier, later):
    return (earlier[0] * later[0], later[0] * earlier[1] + later[1])

def smooth(values):
    return jax.nn.gelu(values, approximate=False)

def gss_layer(resid, norm_gain, norm_bias, gate_mat, value_mat, input_map, decay_rates, output_map, mix_mat, down_mat, keep_row, live_row, reset_row, start_state):
    centre = resid - lax.optimization_barrier(jnp.mean(resid, axis=-1, keepdims=True))
    spread = lax.optimization_barrier(jnp.mean(centre * centre, axis=-1, keepdims=True))
    normed = low(centre * lax.rsqrt(spread + 1e-05) * norm_gain + norm_bias)
    gate_pre = low_back(matmul(normed, gate_mat))
    value_pre = low_back(matmul(normed, value_mat))
    value_act = low(smooth(value_pre))
    driven = low_back(matmul(value_act, input_map))
    retain = jnp.exp(-decay_rates)
    inject = jnp.sqrt(-jnp.expm1(-2.0 * decay_rates))
    live_col = live_row[:, None]
    reset_col = reset_row[:, None]
    factor = jnp.where(reset_col, 0.0, jnp.where(live_col, keep_row[:, None] * retain[None, :], 1.0))
    source = jnp.where(live_col, inject[None, :] * driven, 0.0)
    source = jnp.concatenate([source[:1] + factor[:1] * start_state[None, :], source[1:]], axis=0)
    cumulative, states = lax.associative_scan(chain_step, (factor, source), axis=0)
    piece_last = states[TOK_DEV - 1::TOK_DEV]
    states_low = low(states)
    mixer_out = low(low_back(matmul(states_low, output_map)))
    value_mix = low_back(matmul(mixer_out, mix_mat))
    hidden = low(smooth(gate_pre) * value_mix)
    branch = low_back(matmul(hidden, down_mat))
    return (resid + branch, piece_last)

def reference(inputs, cotangent, lengths, keep, init_states, ln_gain, ln_bias, w_gate, w_value, in_map, rates, out_map, w_mix, w_down):
    weights = (ln_gain.astype(jnp.float32), ln_bias.astype(jnp.float32), w_gate.astype(jnp.float32), w_value.astype(jnp.float32), in_map.astype(jnp.float32), rates.astype(jnp.float32), out_map.astype(jnp.float32), w_mix.astype(jnp.float32), w_down.astype(jnp.float32))
    positions = jnp.arange(ROW, dtype=jnp.int32)
    first_len = lengths[:, 0].astype(jnp.int32)
    second_len = lengths[:, 1].astype(jnp.int32)
    live_all = positions[None, :] < (first_len + second_len)[:, None]
    reset_all = (positions[None, :] == first_len[:, None]) & (second_len[:, None] > 0)
    first_in = inputs.astype(jnp.float32)
    probe = jnp.zeros(first_in.shape, jnp.float32)

    def whole(first_in, probe, weights):
        firsts = []
        seconds = []
        ends_first = []
        ends_second = []
        for row_no in range(MICRO):
            layer_one = [item[0] for item in weights]
            layer_two = [item[1] for item in weights]
            out_one, end_one = gss_layer(first_in[row_no], *layer_one, keep[row_no], live_all[row_no], reset_all[row_no], init_states[0, row_no])
            passed = low_back(low(out_one)) + probe[row_no]
            out_two, end_two = gss_layer(passed, *layer_two, keep[row_no], live_all[row_no], reset_all[row_no], init_states[1, row_no])
            firsts.append(out_one)
            seconds.append(out_two)
            ends_first.append(end_one)
            ends_second.append(end_two)
        second_all = jnp.stack(seconds)
        return (second_all, (jnp.stack(firsts), second_all, jnp.stack([jnp.stack(ends_first), jnp.stack(ends_second)])))
    primal, back_fn, extras = jax.vjp(whole, first_in, probe, weights, has_aux=True)
    grad_first, grad_probe, grad_weights = back_fn(cotangent.astype(jnp.float32))
    block_out = jnp.stack([extras[0], extras[1]]).astype(jnp.bfloat16)
    grad_in = jnp.stack([grad_first, grad_probe])
    return (block_out, grad_in, extras[2], grad_weights[0], grad_weights[1], grad_weights[2], grad_weights[3], grad_weights[4], grad_weights[5], grad_weights[6], grad_weights[7], grad_weights[8])
```

```python
import functools
import math

import jax
import jax.numpy as jnp
from jax import lax
from jax.experimental import pallas as pl
from jax.experimental.pallas import tpu as pltpu
from jax.sharding import PartitionSpec as P

F32 = jnp.float32
BF16 = jnp.bfloat16
VMEM_BYTES = 56 * 1024 * 1024
LANES = 128


def gelu_and_slope(v):
    half_sq = jnp.exp(-0.5 * v * v)
    t = 1.0 / (1.0 + (0.3275911 * 0.7071067811865476) * jnp.abs(v))
    poly = t * (
        0.127414796 + t * (-0.142248368 + t * (0.7107068705 + t * (-0.7265760135 + t * 0.5307027145)))
    )
    tail = poly * half_sq
    cdf = jnp.where(v >= 0.0, 1.0 - tail, tail)
    return v * cdf, cdf + v * half_sq * 0.3989422804014327


def dot(left, right):
    return jnp.dot(left, right, preferred_element_type=F32)


def dot_t(left, right):
    return lax.dot_general(left, right, (((1,), (1,)), ((), ())), preferred_element_type=F32)


def dot_rows(left, right):
    return lax.dot_general(left, right, (((0,), (0,)), ((), ())), preferred_element_type=F32)


def fetch(own, mine, other, window, kept, sem):
    @pl.when(own)
    def _():
        pltpu.make_async_copy(mine.at[window], kept, sem).start()

    @pl.when(jnp.logical_not(own))
    def _():
        pltpu.make_async_copy(other.at[window], kept, sem).start()


def landed(mine, window, kept, sem):
    pltpu.make_async_copy(mine.at[window], kept, sem).wait()


def whole_of(ref):
    return tuple(pl.ds(0, size) for size in ref.shape)


def side_window(ref, axis, side, width):
    start = pl.multiple_of(side * width, LANES)
    return tuple(pl.ds(start, width) if d == axis else pl.ds(0, size) for d, size in enumerate(ref.shape))


def wide(values, width):
    return jnp.concatenate([values] * (width // LANES), axis=1)


def norm_parts(x):
    centre = x - jnp.mean(x, axis=-1, keepdims=True)
    spread = jnp.mean(centre * centre, axis=-1, keepdims=True)
    return centre, lax.rsqrt(spread + 1e-05)


def normed(x, gain_ref, bias_ref):
    centre, rstd = norm_parts(x)
    return (centre * rstd * gain_ref[...] + bias_ref[...]).astype(BF16)


def spread_rows(ref, rows):
    return jnp.broadcast_to(ref[...], (rows, ref.shape[1]))


def at(t, rows):
    return pl.ds(pl.multiple_of(t * rows, rows), rows)


def norm_kernel(layer, flags, x_ref, gain_ref, bias_ref, norm_ref, turned_ref):
    x = jnp.swapaxes(x_ref[...].astype(F32), 0, 1).reshape(norm_ref.shape)
    turned_ref[...] = x.astype(BF16)
    norm_ref[...] = normed(x, gain_ref, bias_ref)


def value_kernel(layer, flags, *refs):
    if layer == 0:
        norm_ref, *refs = refs
    else:
        x_ref, y_ref, z_ref, gain_ref, bias_ref, *refs = refs
    (wv_mine, wv_other, im_mine, im_other, retain_ref, inject_ref, through_ref, dead_ref, *refs) = refs
    if layer == 0:
        act_ref, slope_ref, drive_ref, carry_ref, wv, im, sems = refs
    else:
        act_ref, slope_ref, drive_ref, carry_ref, x1_ref, norm_ref, wv, im, sems = refs
    first = pl.program_id(0) == 0
    own = flags[layer] > 0

    @pl.when(first)
    def _():
        fetch(own, wv_mine, wv_other, whole_of(wv), wv, sems.at[0])
        fetch(own, im_mine, im_other, whole_of(im), im, sems.at[1])

    if layer == 0:
        norm = norm_ref[...]
    else:
        low = (x_ref[...].astype(F32) + (y_ref[...].astype(F32) + z_ref[...].astype(F32))).astype(BF16)
        x1_ref[...] = low
        norm = normed(low.astype(F32), gain_ref, bias_ref)
        norm_ref[...] = norm

    @pl.when(first)
    def _():
        landed(wv_mine, whole_of(wv), wv, sems.at[0])
        landed(im_mine, whole_of(im), im, sems.at[1])

    act, slope = gelu_and_slope(dot(norm, wv[...]))
    act = act.astype(BF16)
    act_ref[...] = act
    slope_ref[...] = slope.astype(BF16)
    drive_ref[...] = dot(act, im[...])
    rows = dead_ref.shape[1]
    width = retain_ref.shape[1]
    retain, inject = spread_rows(retain_ref, rows), spread_rows(inject_ref, rows)

    @pl.when(first)
    def _():
        carry_ref[:rows, :] = jnp.ones((rows, width), F32)
        carry_ref[rows:, :] = jnp.zeros((rows, width), F32)

    def step(t, state):
        through, end = state
        dead = wide(dead_ref[t], width)
        factor = wide(through_ref[t], width) * retain + dead
        return factor * through, factor * end + (1.0 - dead) * inject * drive_ref[at(t, rows), :]

    through, end = lax.fori_loop(
        0, dead_ref.shape[0], step, (carry_ref[:rows, :], carry_ref[rows:, :]), unroll=8
    )
    carry_ref[:rows, :] = through
    carry_ref[rows:, :] = end


def gate_kernel(part, layer, flags, norm_ref, wg_mine, wg_other, act_ref, slope_ref, wg, sems):
    width = wg.shape[1]
    start = pl.multiple_of(flags[2] * (wg_mine.shape[1] // 2) + part * width, LANES)
    window = (pl.ds(0, wg.shape[0]), pl.ds(start, width))

    @pl.when(pl.program_id(0) == 0)
    def _():
        fetch(flags[layer] > 0, wg_mine, wg_other, window, wg, sems.at[0])
        landed(wg_mine, window, wg, sems.at[0])

    act, slope = gelu_and_slope(dot(norm_ref[...], wg[...]))
    act_ref[...] = act.astype(BF16)
    slope_ref[...] = slope.astype(BF16)


def mix_kernel(parts, layer, flags, entry_ref, drive_ref, retain_ref, inject_ref, through_ref, dead_ref, *refs):
    acts, refs = refs[:parts], refs[parts:]
    (
        om_mine, om_other, wm_mine, wm_other, wd_mine, wd_other,
        low_ref, mixer_ref, mix_ref, hidden_ref, branch_ref, om, wm, wd, states, last, sems,
    ) = refs
    first = pl.program_id(0) == 0
    own = flags[layer] > 0
    half = wm.shape[1]
    wm_window = side_window(wm_mine, 1, flags[2], half)
    wd_window = side_window(wd_mine, 0, flags[2], half)

    @pl.when(first)
    def _():
        fetch(own, om_mine, om_other, whole_of(om), om, sems.at[0])
        fetch(own, wm_mine, wm_other, wm_window, wm, sems.at[1])
        fetch(own, wd_mine, wd_other, wd_window, wd, sems.at[2])
        last[...] = entry_ref[...]

    rows = dead_ref.shape[1]
    width = retain_ref.shape[1]
    retain, inject = spread_rows(retain_ref, rows), spread_rows(inject_ref, rows)

    def step(t, state):
        dead = wide(dead_ref[t], width)
        factor = wide(through_ref[t], width) * retain + dead
        state = factor * state + (1.0 - dead) * inject * drive_ref[at(t, rows), :]
        states[at(t, rows), :] = state
        return state

    last[...] = lax.fori_loop(0, dead_ref.shape[0], step, last[...], unroll=8)
    low = states[...].astype(BF16)
    low_ref[...] = low

    @pl.when(first)
    def _():
        landed(om_mine, whole_of(om), om, sems.at[0])
        landed(wm_mine, wm_window, wm, sems.at[1])
        landed(wd_mine, wd_window, wd, sems.at[2])

    mixer = dot(low, om[...]).astype(BF16)
    mixer_ref[...] = mixer
    step_width = half // parts
    branch = None
    for i, act_ref in enumerate(acts):
        here = slice(i * step_width, (i + 1) * step_width)
        value_mix = dot(mixer, wm[:, here])
        mix_ref[:, here] = value_mix.astype(BF16)
        hidden = (act_ref[...].astype(F32) * value_mix).astype(BF16)
        hidden_ref[:, here] = hidden
    branch_ref[...] = dot(hidden_ref[...], wd[...]).astype(BF16)


def middle_kernel(
    parts, layer, flags, entry_ref, drive_ref, grad_ref, retain_ref, inject_ref, through_ref, dead_ref, *refs
):
    acts, slopes, refs = refs[:parts], refs[parts : 2 * parts], refs[2 * parts :]
    (
        om_mine, om_other, wm_mine, wm_other, wd_mine, wd_other,
        low_ref, mixer_ref, hidden_ref, branch_ref, gate_low_ref, mix_low_ref, mixer_back_ref,
        om, wm, wd, states, last, sems,
    ) = refs
    first = pl.program_id(0) == 0
    own = flags[layer] > 0
    half = wm.shape[1]
    wm_window = side_window(wm_mine, 1, flags[2], half)
    wd_window = side_window(wd_mine, 0, flags[2], half)

    @pl.when(first)
    def _():
        fetch(own, om_mine, om_other, whole_of(om), om, sems.at[0])
        fetch(own, wm_mine, wm_other, wm_window, wm, sems.at[1])
        fetch(own, wd_mine, wd_other, wd_window, wd, sems.at[2])
        last[...] = entry_ref[...]

    rows = dead_ref.shape[1]
    width = retain_ref.shape[1]
    retain, inject = spread_rows(retain_ref, rows), spread_rows(inject_ref, rows)

    def step(t, state):
        dead = wide(dead_ref[t], width)
        factor = wide(through_ref[t], width) * retain + dead
        state = factor * state + (1.0 - dead) * inject * drive_ref[at(t, rows), :]
        states[at(t, rows), :] = state
        return state

    last[...] = lax.fori_loop(0, dead_ref.shape[0], step, last[...], unroll=8)
    low = states[...].astype(BF16)
    low_ref[...] = low

    @pl.when(first)
    def _():
        landed(om_mine, whole_of(om), om, sems.at[0])
        landed(wm_mine, wm_window, wm, sems.at[1])
        landed(wd_mine, wd_window, wd, sems.at[2])

    mixer = dot(low, om[...]).astype(BF16)
    mixer_ref[...] = mixer
    step_width = half // parts
    for i in range(parts):
        here = slice(i * step_width, (i + 1) * step_width)
        value_mix = dot(mixer, wm[:, here])
        act = acts[i][...].astype(F32)
        hidden_ref[:, here] = (act * value_mix).astype(BF16)
        d_hidden = dot_t(grad_ref[...], wd[here, :])
        gate_low_ref[:, here] = (slopes[i][...].astype(F32) * (d_hidden * value_mix)).astype(BF16)
        mix_low_ref[:, here] = (d_hidden * act).astype(BF16)
    mixer_back_ref[...] = dot_t(mix_low_ref[...], wm[...]).astype(BF16)
    branch_ref[...] = dot(hidden_ref[...], wd[...]).astype(BF16)


def hidden_back_kernel(parts, layer, flags, grad_ref, mix_ref, *refs):
    acts, slopes, refs = refs[:parts], refs[parts : 2 * parts], refs[2 * parts :]
    wd_mine, wd_other, wm_mine, wm_other, gate_low_ref, mix_low_ref, mixer_ref, wd, wm, sems = refs
    own = flags[layer] > 0
    half = wm.shape[1]
    wm_window = side_window(wm_mine, 1, flags[2], half)
    wd_window = side_window(wd_mine, 0, flags[2], half)

    @pl.when(pl.program_id(0) == 0)
    def _():
        fetch(own, wd_mine, wd_other, wd_window, wd, sems.at[0])
        fetch(own, wm_mine, wm_other, wm_window, wm, sems.at[1])
        landed(wd_mine, wd_window, wd, sems.at[0])
        landed(wm_mine, wm_window, wm, sems.at[1])

    step_width = half // parts
    for i in range(parts):
        here = slice(i * step_width, (i + 1) * step_width)
        d_hidden = dot_t(grad_ref[...], wd[here, :])
        gate_low_ref[:, here] = (
            slopes[i][...].astype(F32) * (d_hidden * mix_ref[:, here].astype(F32))
        ).astype(BF16)
        mix_low_ref[:, here] = (d_hidden * acts[i][...].astype(F32)).astype(BF16)
    mixer_ref[...] = dot_t(mix_low_ref[...], wm[...]).astype(BF16)


def states_back_kernel(
    layer, flags, mixer_ref, mixer_other, retain_ref, through_ref, dead_ref, om_mine, om_other,
    mixer_low_ref, d_states_ref, carry_ref, om, sems,
):
    first = pl.program_id(0) == 0
    rows = dead_ref.shape[1]
    count = dead_ref.shape[0]
    width = retain_ref.shape[1]

    @pl.when(first)
    def _():
        fetch(flags[layer] > 0, om_mine, om_other, whole_of(om), om, sems.at[0])
        carry_ref[:rows, :] = jnp.ones((rows, width), F32)
        carry_ref[rows:, :] = jnp.zeros((rows, width), F32)
        landed(om_mine, whole_of(om), om, sems.at[0])

    low = (mixer_ref[...].astype(F32) + mixer_other[...].astype(F32)).astype(BF16)
    mixer_low_ref[...] = low
    d_states_ref[...] = dot_t(low, om[...])
    retain = spread_rows(retain_ref, rows)

    def step(i, state):
        t = count - 1 - i
        through, end = state
        factor = wide(through_ref[t], width) * retain + wide(dead_ref[t], width)
        return factor * through, factor * (end + d_states_ref[at(t, rows), :])

    through, end = lax.fori_loop(0, count, step, (carry_ref[:rows, :], carry_ref[rows:, :]), unroll=8)
    carry_ref[:rows, :] = through
    carry_ref[rows:, :] = end


def drive_back_kernel(
    layer, flags, back_ref, entry_ref, d_states_ref, states_ref, drive_ref, retain_ref, inject_ref, gain_ref,
    through_ref, dead_ref, slope_ref, im_mine, im_other,
    drive_low_ref, value_low_ref, rate_ref, im, states, d_drive, kept, sems,
):
    block = pl.program_id(0)
    rows = dead_ref.shape[1]
    count = dead_ref.shape[0]
    width = retain_ref.shape[1]

    @pl.when(block == 0)
    def _():
        fetch(flags[layer] > 0, im_mine, im_other, whole_of(im), im, sems.at[0])
        kept[0] = back_ref[...]
        kept[1] = jnp.zeros((rows, width), F32)
        kept[2] = jnp.zeros((rows, width), F32)
        kept[3] = jnp.zeros((rows, width), F32)
        landed(im_mine, whole_of(im), im, sems.at[0])

    retain, inject = spread_rows(retain_ref, rows), spread_rows(inject_ref, rows)
    states[...] = states_ref[...].astype(F32)

    def step(i, state):
        carried, flow, decay_sum, inject_sum = state
        t = count - 1 - i
        here = at(t, rows)
        dead = wide(dead_ref[t], width)
        lam = d_states_ref[here, :] + carried
        decay_sum = decay_sum + flow * states[here, :]
        alive = (1.0 - dead) * lam
        d_drive[here, :] = alive * inject
        inject_sum = inject_sum + alive * drive_ref[here, :]
        flow = wide(through_ref[t], width) * lam
        return flow * retain + dead * lam, flow, decay_sum, inject_sum

    carried, flow, decay_sum, inject_sum = lax.fori_loop(
        0, count, step, (kept[0], kept[1], kept[2], kept[3]), unroll=8
    )
    kept[0] = carried
    kept[1] = flow
    kept[2] = decay_sum
    kept[3] = inject_sum

    @pl.when(block == pl.num_programs(0) - 1)
    def _():
        rate_ref[...] = jnp.sum(
            gain_ref[...] * inject_sum - retain * (decay_sum + flow * entry_ref[...]), axis=0, keepdims=True
        )

    low = d_drive[...].astype(BF16)
    drive_low_ref[...] = low
    value_low_ref[...] = (slope_ref[...].astype(F32) * dot_t(low, im[...])).astype(BF16)


def gate_back_kernel(layer, flags, gate_low_ref, wg_mine, wg_other, d_norm_ref, wg, sems):
    window = side_window(wg_mine, 1, flags[2], wg.shape[1])

    @pl.when(pl.program_id(0) == 0)
    def _():
        fetch(flags[layer] > 0, wg_mine, wg_other, window, wg, sems.at[0])
        landed(wg_mine, window, wg, sems.at[0])

    d_norm_ref[...] = dot_t(gate_low_ref[...], wg[...]).astype(BF16)


def norm_back_kernel(
    layer, flags, grad_ref, d_norm_ref, d_norm_other, value_low_ref, x_ref, gain_ref, wv_mine, wv_other,
    d_x_ref, d_x_low_ref, vector_ref, wv, sems,
):
    @pl.when(pl.program_id(0) == 0)
    def _():
        fetch(flags[layer] > 0, wv_mine, wv_other, whole_of(wv), wv, sems.at[0])
        vector_ref[...] = jnp.zeros_like(vector_ref)
        landed(wv_mine, whole_of(wv), wv, sems.at[0])

    d_norm = (d_norm_ref[...].astype(F32) + d_norm_other[...].astype(F32)) + dot_t(value_low_ref[...], wv[...])
    centre, rstd = norm_parts(x_ref[...].astype(F32))
    xhat = centre * rstd
    vector_ref[0:1, :] += jnp.sum(d_norm * xhat, axis=0, keepdims=True)
    vector_ref[1:2, :] += jnp.sum(d_norm, axis=0, keepdims=True)
    scaled = d_norm * gain_ref[...]
    first = jnp.mean(scaled, axis=-1, keepdims=True)
    second = jnp.mean(scaled * xhat, axis=-1, keepdims=True)
    d_x = grad_ref[...].astype(F32) + (scaled - first - xhat * second) * rstd
    d_x_ref[...] = d_x
    d_x_low_ref[...] = d_x.astype(BF16)


def shape(dims, dtype):
    return jax.ShapeDtypeStruct(dims, dtype)


def run(kernel, flags, grid, operands, outs, scratch, flops=0):
    arrays = [array for array, _ in operands]
    held = 6 * 1024 * 1024
    for array, spec in operands + outs:
        if spec.block_shape is not None:
            held += 2 * math.prod(spec.block_shape) * array.dtype.itemsize
    for item in scratch:
        if item.dtype in (F32, BF16):
            held += math.prod(item.shape) * item.dtype.itemsize
    return pl.pallas_call(
        kernel,
        out_shape=[struct for struct, _ in outs],
        grid_spec=pltpu.PrefetchScalarGridSpec(
            num_scalar_prefetch=1,
            grid=grid,
            in_specs=[spec for _, spec in operands],
            out_specs=[spec for _, spec in outs],
            scratch_shapes=scratch,
        ),
        cost_estimate=pl.CostEstimate(flops=0, bytes_accessed=0, transcendentals=0),
        compiler_params=pltpu.CompilerParams(
            vmem_limit_bytes=held, dimension_semantics=("arbitrary",) * len(grid)
        ),
    )(flags, *arrays)


def far(array):
    return pltpu.with_memory_space_constraint(array, pltpu.HBM)


def whole(dims):
    return pl.BlockSpec(dims, lambda *_: (0,) * len(dims))


class Reduction:
    def __init__(self, arrays, bits, mine):
        self.left = tuple(sorted(bits, reverse=True))
        self.terms = [(tuple(arrays), self.left)]
        self.fixed = {}
        self.mine = mine

    def part(self, fixed):
        left = [bit for bit in self.left if bit not in fixed]
        total = None
        for arrays, bits in self.terms:
            pieces = []
            for array in arrays:
                block = array.shape[len(bits) :]
                starts = [fixed.get(bit, 0) for bit in bits] + [0] * len(block)
                sizes = [1 if bit in fixed else 2 for bit in bits] + list(block)
                pieces.append(lax.dynamic_slice(array, starts, sizes).reshape((2,) * len(left) + tuple(block)))
            term = pieces[0] if len(pieces) == 1 else jnp.concatenate(pieces, axis=-2)
            term = term.astype(F32)
            total = term if total is None else total + term
        return total

    def message(self, bit):
        away = dict(self.fixed)
        away[bit] = 1 - self.mine[bit]
        return self.part(away).astype(BF16)

    def step(self, bit):
        self.send(bit, self.message(bit))

    def send(self, bit, sent):
        count = lax.axis_size("seq")
        self.take(bit, lax.ppermute(sent, "seq", [(i, i ^ (1 << bit)) for i in range(count)]))

    def take(self, bit, came):
        self.fixed[bit] = self.mine[bit]
        self.terms.append(((came,), tuple(b for b in self.left if b not in self.fixed)))

    def result(self):
        return self.part(self.fixed)


def carried(pieces, mine, backward, anchor=None, fillers=(), sends=(), late=None):
    rows = pieces.shape[0] // 2
    count = lax.axis_size("seq")
    through, end = pieces[:rows], pieces[rows:]
    before_through, before_end = jnp.ones_like(through), jnp.zeros_like(end)
    filled = []
    for bit in range(len(mine)):
        message = jnp.concatenate([through, end], axis=0)
        if bit < len(fillers):
            message, anchor, filled = lax.optimization_barrier((message, anchor, filled))
        if late is not None and bit == len(fillers) - 1:
            message, late = lax.optimization_barrier((message, late))
            anchor = (anchor, late)
        came = lax.ppermute(message, "seq", [(i, i ^ (1 << bit)) for i in range(count)])
        if bit < len(sends) and sends[bit] is not None:
            sends[bit](filled)
        if bit < len(fillers):
            filled = filled + [fillers[bit](anchor, filled)]
            came, filled = lax.optimization_barrier((came, filled))
        far_through, far_end = came[:rows], came[rows:]
        first = mine[bit] == (0 if backward else 1)
        before_end = jnp.where(first, before_through * far_end + before_end, before_end)
        before_through = jnp.where(first, before_through * far_through, before_through)
        end = jnp.where(first, through * far_end + end, far_through * end + far_end)
        through = through * far_through
    for filler in fillers[len(mine) :]:
        filled = filled + [filler(anchor, filled)]
    return before_through, before_end, filled


def swap(array):
    return lax.ppermute(array, "section", [(0, 1), (1, 0)])


def on_device(
    inputs, cotangent, lengths, keep, init_states, ln_gain, ln_bias, w_gate, w_value, in_map, rates, out_map,
    w_mix, w_down,
):
    rows, count, width = inputs.shape
    tokens = rows * count
    gate_width = w_gate.shape[2]
    half = gate_width // 2
    value_width = w_value.shape[2]
    state_width = in_map.shape[2]
    section = lax.axis_index("section")
    piece = lax.axis_index("seq")
    pieces = lax.axis_size("seq")
    bits = pieces.bit_length() - 1
    mine = [(piece >> bit) & 1 for bit in range(bits)]
    block = 256 if tokens % 256 == 0 else tokens
    grid = (tokens // block,)
    parts = 4

    any_spec = pl.BlockSpec(memory_space=pl.ANY)

    def pair(mine, other):
        return [(far(mine), any_spec), (far(other), any_spec)]

    my_vectors = jnp.concatenate([ln_gain[0], ln_bias[0], rates[0], init_states[0].reshape(-1)])
    vectors = swap(my_vectors)
    wv_other, im_other = swap(w_value[0]), swap(in_map[0])
    wv, im = pair(w_value[0], wv_other), pair(in_map[0], im_other)
    wg_mine, inputs, _, _ = lax.optimization_barrier((w_gate[0], inputs, wv_other, im_other))
    wg = pair(wg_mine, swap(wg_mine))
    flags = jnp.stack([(section == 0).astype(jnp.int32), (section == 1).astype(jnp.int32), section.astype(jnp.int32)])

    grad_top = cotangent.transpose(1, 0, 2).reshape(tokens, width)

    positions = piece * count + jnp.arange(count, dtype=jnp.int32)
    first_len, second_len = lengths[:, 0][None, :], lengths[:, 1][None, :]
    live = positions[:, None] < first_len + second_len
    reset = (positions[:, None] == first_len) & (second_len > 0)
    through = jnp.where(live & jnp.logical_not(reset), keep.T, 0.0)
    dead = jnp.where(live, 0.0, 1.0).astype(F32)
    through = jnp.broadcast_to(through[:, :, None], (count, rows, LANES))
    dead = jnp.broadcast_to(dead[:, :, None], (count, rows, LANES))
    mask_dims = (block // rows, rows, LANES)
    end_block = grid[0] - 1
    mask_spec = pl.BlockSpec(mask_dims, lambda i, f: (i, 0, 0))
    back_mask_spec = pl.BlockSpec(mask_dims, lambda i, f: (end_block - i, 0, 0))
    masks = [(through, mask_spec), (dead, mask_spec)]
    back_masks = [(through, back_mask_spec), (dead, back_mask_spec)]

    def by_rows(cols):
        return pl.BlockSpec((block, cols), lambda i, f: (i, 0))

    def by_rows_back(cols):
        return pl.BlockSpec((block, cols), lambda i, f: (end_block - i, 0))

    def out(cols, dtype=BF16, back=False):
        struct = pltpu.HBM((tokens, cols), dtype)
        return (struct, by_rows_back(cols) if back else by_rows(cols))

    def sems(n):
        return pltpu.SemaphoreType.DMA((n,))

    carry_dims = (2 * rows, state_width)
    carry_out = (shape(carry_dims, F32), whole(carry_dims))
    row_state = whole((rows, state_width))
    wv_dims, im_dims, om_dims = (width, value_width), (value_width, state_width), (state_width, value_width)
    wg_dims, wm_dims, wd_dims = (width, half), (value_width, half), (half, width)

    layers = []
    for layer in range(2):
        chosen = jnp.where(section == layer, my_vectors, vectors)
        gain, bias, rate = (
            chosen[:width][None],
            chosen[width : 2 * width][None],
            chosen[2 * width : 2 * width + state_width][None],
        )
        start = chosen[2 * width + state_width :].reshape(rows, state_width)
        inject = jnp.sqrt(-jnp.expm1(-2.0 * rate))
        one_width, one_state = whole((1, width)), whole((1, state_width))
        layers.append(
            dict(
                gain=(gain, one_width),
                bias=(bias, one_width),
                retain=(jnp.exp(-rate), one_state),
                inject=(inject, one_state),
                rate_gain=(jnp.exp(-2.0 * rate) / inject, one_state),
                start=start,
            )
        )

    saved = []
    ends = []
    branch = None
    for layer in range(2):
        now = layers[layer]
        outs = [out(value_width), out(value_width), out(state_width, F32), carry_out]
        if layer == 0:
            by_positions = pl.BlockSpec((rows, block // rows, width), lambda i, f: (0, i, 0))
            norm, x0 = run(
                functools.partial(norm_kernel, layer),
                flags,
                grid,
                [(far(inputs), by_positions), now["gain"], now["bias"]],
                [out(width), out(width)],
                [],
            )
            x = x0
            sources = [(norm, by_rows(width))]
        else:
            sources = [
                (far(x0), by_rows(width)), (far(branch), by_rows(width)), (far(swap(branch)), by_rows(width)),
                now["gain"], now["bias"],
            ]
            outs += [out(width), out(width)]
        value_act, value_slope, drive, pieces_map, *more = run(
            functools.partial(value_kernel, layer),
            flags,
            grid,
            sources + wv + im + [now["retain"], now["inject"]] + masks,
            outs,
            [pltpu.VMEM(wv_dims, BF16), pltpu.VMEM(im_dims, BF16), sems(2)],
            flops=2 * tokens * (width * value_width + value_width * state_width),
        )
        if more:
            x, norm = more
        if layer == 0:
            pieces_map, *rest = lax.optimization_barrier((pieces_map, out_map[0], w_mix[0], w_down[0]))
            om, wm, wd = (pair(array, swap(array)) for array in rest)

        def gate_part(norm, filled, part, layer=layer):
            cols = half // parts
            return run(
                functools.partial(gate_kernel, part, layer),
                flags,
                grid,
                [(norm, by_rows(width))] + wg,
                [out(cols)] * 2,
                [pltpu.VMEM((width, cols), BF16), sems(1)],
                flops=2 * tokens * width * cols,
            )

        before_through, before_end, gates = carried(
            pieces_map, mine, False, norm, [functools.partial(gate_part, part=part) for part in range(parts)]
        )
        gate_act = [act for act, _ in gates]
        gate_slope = [slope for _, slope in gates]
        entry = before_through * now["start"] + before_end
        ends.append(pieces_map[:rows] * entry + pieces_map[rows:])
        if layer == 0:
            states_low, mixer, value_mix, hidden, branch = run(
                functools.partial(mix_kernel, parts, layer),
                flags,
                grid,
                [(entry, row_state), (drive, by_rows(state_width)), now["retain"], now["inject"]]
                + masks
                + [(act, by_rows(half // parts)) for act in gate_act]
                + om
                + wm
                + wd,
                [out(cols) for cols in (state_width, value_width, half, half, width)],
                [
                    pltpu.VMEM(om_dims, BF16),
                    pltpu.VMEM(wm_dims, BF16),
                    pltpu.VMEM(wd_dims, BF16),
                    pltpu.VMEM((block, state_width), F32),
                    pltpu.VMEM((rows, state_width), F32),
                    sems(3),
                ],
                flops=2 * tokens * (state_width * value_width + value_width * half + half * width),
            )
        else:
            value_mix = None
            states_low, mixer, hidden, branch, gate_low, mix_low, mixer_part = run(
                functools.partial(middle_kernel, parts, layer),
                flags,
                grid,
                [
                    (entry, row_state), (drive, by_rows(state_width)), (far(grad_top), by_rows(width)),
                    now["retain"], now["inject"],
                ]
                + masks
                + [(array, by_rows(half // parts)) for array in gate_act + gate_slope]
                + om
                + wm
                + wd,
                [
                    out(state_width), out(value_width), out(half), out(width), out(half), out(half),
                    out(value_width),
                ],
                [
                    pltpu.VMEM(om_dims, BF16),
                    pltpu.VMEM(wm_dims, BF16),
                    pltpu.VMEM(wd_dims, BF16),
                    pltpu.VMEM((block, state_width), F32),
                    pltpu.VMEM((rows, state_width), F32),
                    sems(3),
                ],
                flops=2 * tokens * (state_width * value_width + 2 * value_width * half + 2 * half * width),
            )
        saved.append(
            dict(
                x=x, norm=norm, value_act=value_act, value_slope=value_slope, drive=drive, gate_act=gate_act,
                gate_slope=gate_slope, entry=entry, states_low=states_low, mixer=mixer,
                value_mix=value_mix, hidden=hidden,
            )
        )
    x1 = saved[1]["x"]

    def gate_norm_part(layer, gate_low):
        return run(
            functools.partial(gate_back_kernel, layer),
            flags,
            grid,
            [(gate_low, by_rows(half))] + wg,
            [out(width)],
            [pltpu.VMEM(wg_dims, BF16), sems(1)],
            flops=2 * tokens * half * width,
        )[0]

    def hidden_back(layer, grad):
        kept = saved[layer]
        return run(
            functools.partial(hidden_back_kernel, parts, layer),
            flags,
            grid,
            [(grad, by_rows(width)), (far(kept["value_mix"]), by_rows(half))]
            + [(far(array), by_rows(half // parts)) for array in kept["gate_act"] + kept["gate_slope"]]
            + wd
            + wm,
            [out(half), out(half), out(value_width)],
            [pltpu.VMEM(wd_dims, BF16), pltpu.VMEM(wm_dims, BF16), sems(2)],
            flops=2 * tokens * half * (width + value_width),
        )

    def states_back(layer, mixer_part, mixer_other):
        return run(
            functools.partial(states_back_kernel, layer),
            flags,
            grid,
            [
                (far(mixer_part), by_rows_back(value_width)),
                (far(mixer_other), by_rows_back(value_width)),
                layers[layer]["retain"],
            ]
            + back_masks
            + om,
            [out(value_width, back=True), out(state_width, F32, back=True), carry_out],
            [pltpu.VMEM(om_dims, BF16), sems(1)],
            flops=2 * tokens * state_width * value_width,
        )

    def drive_back(layer, back, d_states):
        now, kept = layers[layer], saved[layer]
        return run(
            functools.partial(drive_back_kernel, layer),
            flags,
            grid,
            [
                (back, row_state),
                (kept["entry"], row_state),
                (d_states, by_rows_back(state_width)),
                (far(kept["states_low"]), by_rows_back(state_width)),
                (far(kept["drive"]), by_rows_back(state_width)),
                now["retain"],
                now["inject"],
                now["rate_gain"],
            ]
            + back_masks
            + [(far(kept["value_slope"]), by_rows_back(value_width))]
            + im,
            [
                out(state_width, back=True),
                out(value_width, back=True),
                (shape((1, state_width), F32), whole((1, state_width))),
            ],
            [
                pltpu.VMEM(im_dims, BF16),
                pltpu.VMEM((block, state_width), F32),
                pltpu.VMEM((block, state_width), F32),
                pltpu.VMEM((4, rows, state_width), F32),
                sems(1),
            ],
            flops=2 * tokens * state_width * value_width,
        )

    def norm_back(layer, grad, d_norm_part, d_norm_other, value_low):
        return run(
            functools.partial(norm_back_kernel, layer),
            flags,
            grid,
            [
                (far(grad), by_rows(width)),
                (far(d_norm_part), by_rows(width)),
                (far(d_norm_other), by_rows(width)),
                (value_low, by_rows(value_width)),
                (far(saved[layer]["x"]), by_rows(width)),
                layers[layer]["gain"],
            ]
            + wv,
            [
                out(width, F32),
                out(width),
                (shape((8, width), F32), whole((8, width))),
            ],
            [pltpu.VMEM(wv_dims, BF16), sems(1)],
            flops=2 * tokens * value_width * width,
        )

    def reductions(d_down, d_gate, d_mix):
        return (
            Reduction([d_down.reshape((2,) * (bits - 1) + (-1, width))], range(bits - 1), mine),
            Reduction([d_gate.reshape((2,) * bits + (-1, half))], range(bits), mine),
            Reduction([d_mix.reshape((2,) * bits + (-1, half))], range(bits), mine),
        )

    cols = value_width // 2

    def sides(layer, value_low, drive_low, mixer_low):
        def my_side(array):
            return lax.dynamic_slice(array, (0, section * cols), (tokens, cols))

        return [
            dot_rows(left, my_side(right)).astype(BF16)
            for left, right in (
                (saved[layer]["norm"], value_low),
                (saved[layer]["value_act"], drive_low),
                (saved[layer]["states_low"], mixer_low),
            )
        ]

    def vector_of(norm_vectors, grad_rate):
        vector = jnp.concatenate(
            [
                norm_vectors[0].reshape(pieces, -1),
                norm_vectors[1].reshape(pieces, -1),
                grad_rate.reshape(pieces, -1),
            ],
            axis=1,
        ).astype(BF16)
        return jnp.pad(vector[:, None, :], ((0, 0), (0, 15), (0, cols - vector.shape[1])))

    def small_of(side_grads, norm_vectors, grad_rate):
        vector = vector_of(norm_vectors, grad_rate)
        arrays = [array.reshape(pieces, -1, cols) for array in side_grads] + [vector]
        (joint,) = tied(jnp.concatenate(arrays, axis=1))
        return joint.reshape((2,) * bits + joint.shape[1:])

    def tied(*arrays):
        return lax.optimization_barrier(arrays)

    def together(reductions, bit):
        messages = [part.message(bit) for part in reductions]
        came = lax.ppermute(
            jnp.concatenate(messages, axis=-2), "seq", [(i, i ^ (1 << bit)) for i in range(pieces)]
        )
        at_row = 0
        for part, message in zip(reductions, messages):
            part.take(bit, came[..., at_row : at_row + message.shape[-2], :])
            at_row += message.shape[-2]

    def arrived(reductions):
        return [part.terms[-1][0] for part in reductions]

    def put_back(reductions, arrays):
        for part, array in zip(reductions, arrays):
            part.terms[-1] = (array, part.terms[-1][1])

    share = value_width // pieces
    order = list(range(bits - 1))
    down_order = order
    gate_order = order[1:2] + order[:1] + order[2:]
    mix_order = order[-1:] + order[:-1]
    small_order = [*gate_order, bits - 1]
    orders = (down_order, gate_order, mix_order)

    def back_carry(layer, back_map, d_down, grads, last=None, late=None):
        parts_ = [Reduction([d_down.reshape((2,) * (bits - 1) + (-1, width))], range(bits - 1), mine)]

        def gate_filler(a, filled):
            return dot_rows(a[0], a[1]).astype(BF16), parts_[0].message(down_order[0])

        def norm_filler(a, filled):
            gate = Reduction([filled[0][0].reshape((2,) * bits + (-1, half))], range(bits), mine)
            parts_.append(gate)
            return gate_norm_part(layer, a[1]), gate.message(gate_order[0])

        def mix_filler(a, filled):
            mix = Reduction(
                [dot_rows(a[2], a[3]).astype(BF16).reshape((2,) * bits + (-1, half))], range(bits), mine
            )
            parts_.append(mix)
            return mix.message(mix_order[0])

        fillers = [gate_filler, norm_filler, mix_filler]
        if last is not None:
            fillers.append(last)
        sends = [
            None,
            lambda filled: parts_[0].send(down_order[0], filled[0][1]),
            lambda filled: parts_[1].send(gate_order[0], filled[1][1]),
        ]
        _, back, filled = carried(back_map, mine, True, grads, fillers, sends, late)
        parts_[2].send(mix_order[0], filled[2])
        return back, filled[1][0], parts_, filled[3:]

    kept = saved[1]
    mixer_other = swap(mixer_part)
    d_down = dot_rows(kept["hidden"], grad_top).astype(BF16)
    mixer_low, d_states, back_map = states_back(1, mixer_part, mixer_other)
    back_map, d_down = tied(back_map, d_down)
    back, d_norm_part, ones, _ = back_carry(1, back_map, d_down, (kept["norm"], gate_low, kept["mixer"], mix_low))
    d_norm_other = swap(d_norm_part)
    drive_low, value_low, grad_rate = drive_back(1, back, d_states)
    d_x1, grad, norm_vectors = norm_back(1, grad_top, d_norm_part, d_norm_other, value_low)
    side_args = (value_low, drive_low, mixer_low)
    tail_one = (norm_vectors, grad_rate)

    kept = saved[0]
    gate_low, mix_low, mixer_part = hidden_back(0, grad)
    mixer_other = swap(mixer_part)
    d_down = dot_rows(kept["hidden"], grad).astype(BF16)
    d_down, *came = tied(d_down, *arrived(ones))
    put_back(ones, came)
    sent = [part.message(order_[1]) for part, order_ in zip(ones, orders)] if len(order) > 1 else []
    mixer_part, mixer_other, d_down, *sent = tied(mixer_part, mixer_other, d_down, *sent)
    for part, order_, message in zip(ones, orders, sent):
        part.send(order_[1], message)
    mixer_low, d_states, back_map = states_back(0, mixer_part, mixer_other)
    back_map, d_down = tied(back_map, d_down)
    def last_filler(a, filled):
        a, came = a
        put_back(ones, came)
        messages = [part.message(order_[2]) for part, order_ in zip(ones, orders)] if len(order) > 2 else []
        return sides(1, *a[4]), messages

    back, d_norm_part, zeros, more = back_carry(
        0,
        back_map,
        d_down,
        (kept["norm"], gate_low, kept["mixer"], mix_low, side_args),
        last_filler,
        arrived(ones),
    )
    sides_one, sent = more[0]
    for part, order_, message in zip(ones, orders, sent):
        part.send(order_[2], message)
    d_norm_other = swap(d_norm_part)
    drive_low, value_low, grad_rate = drive_back(0, back, d_states)
    d_x0, _, norm_vectors = norm_back(0, grad, d_norm_part, d_norm_other, value_low)
    norm_vectors, *came = tied(norm_vectors, *arrived(zeros))
    put_back(zeros, came)
    sent = [part.message(order_[1]) for part, order_ in zip(zeros, orders)] if len(order) > 1 else []
    small_one = small_of(sides_one, *tail_one)
    norm_vectors, small_one, *sent = tied(norm_vectors, small_one, *sent)
    for part, order_, message in zip(zeros, orders, sent):
        part.send(order_[1], message)
    sides_zero = sides(0, value_low, drive_low, mixer_low)
    small_zero = small_of(sides_zero, norm_vectors, grad_rate)
    small_zero, *came = tied(small_zero, *arrived(ones))
    put_back(ones, came)
    for place in range(3, bits - 1):
        for part, order_ in zip(ones, orders):
            part.step(order_[place])
    together(ones[1:], bits - 1)
    small = Reduction([small_one, small_zero], range(bits), mine)
    small.step(small_order[0])
    for place in range(2, bits - 1):
        zero_last = tied(*arrived(zeros), *arrived(ones[1:]))
        put_back((*zeros, *ones[1:]), zero_last)
        for part, order_ in zip(zeros, orders):
            part.step(order_[place])
        small.step(small_order[place - 1])
    together(zeros[1:], bits - 1)
    small.step(small_order[bits - 2])
    small.step(bits - 1)
    small = small.result()
    reduced = [None, None]
    for layer, (down, gate, mix) in ((1, ones), (0, zeros)):
        top = pieces // 2
        part = down.result()
        sent = part.astype(BF16)
        mate = 1 - layer
        across = [
            pair
            for low in range(top)
            for pair in (
                (layer * pieces + mate * top + low, layer * pieces + layer * top + low),
                (mate * pieces + layer * top + low, layer * pieces + mate * top + low),
            )
        ]
        beside = [(mate * pieces + mate * top + low, layer * pieces + mate * top + low) for low in range(top)]
        came = lax.ppermute(sent, ("section", "seq"), across).astype(F32)
        came = came + lax.ppermute(sent, ("section", "seq"), beside).astype(F32)
        reduced[layer] = [jnp.where(mine[bits - 1] == layer, part, 0.0) + came, gate.result(), mix.result()]
    each = small.shape[0] // 2
    reduced[1].append(small[:each])
    reduced[0].append(small[each:])
    d_xs = [d_x0, d_x1]

    branch, _ = tied(branch, d_x0)
    branch_other = swap(branch)
    second_out = (x1.astype(F32) + (branch.astype(F32) + branch_other.astype(F32))).astype(BF16)
    block_out = jnp.where(section == 0, x1, second_out)

    keep_own = [jnp.where(section == 0, a, b) for a, b in zip(reduced[0], reduced[1])]
    give = [jnp.where(section == 0, b, a).astype(BF16) for a, b in zip(reduced[0][1:], reduced[1][1:])]
    taken_wide = swap(jnp.concatenate(give[:2], axis=0))
    taken_small = swap(give[2]).astype(F32)
    cut = give[0].shape[0]
    taken = [taken_wide[:cut].astype(F32), taken_wide[cut:].astype(F32)]

    def joined(own, other):
        return jnp.where(
            section == 0, jnp.concatenate([own, other], axis=-1), jnp.concatenate([other, own], axis=-1)
        )

    grad_down = keep_own[0]
    grad_gate = joined(keep_own[1], taken[0])
    grad_mix = joined(keep_own[2], taken[1])
    small = joined(keep_own[3], taken_small)
    part = width // pieces
    grad_value, grad_input, grad_output = small[:part], small[part : part + share], small[part + share : part + 2 * share]
    vector = keep_own[3][part + 2 * share]
    grad_gain, grad_bias = vector[:part], vector[part : 2 * part]
    grad_rates = vector[2 * part : 2 * part + state_width // pieces]
    grad_in = jnp.where(section == 0, d_xs[0], d_xs[1])
    end_states = jnp.where(section == 0, ends[0], ends[1])

    def by_row(array):
        return array.reshape(count, rows, width).transpose(1, 0, 2)[None]

    return (
        by_row(block_out),
        by_row(grad_in),
        end_states[None, :, None, :],
        grad_gain[None],
        grad_bias[None],
        grad_gate[None],
        grad_value[None],
        grad_input[None],
        grad_rates[None],
        grad_output[None],
        grad_mix[None],
        grad_down[None],
    )


def solution(mesh):
    in_specs = (
        P(None, "seq", None),
        P(None, "seq", None),
        P(),
        P(None, "seq"),
        P("section", None, None),
        P("section", None),
        P("section", None),
        P("section", None, None),
        P("section", None, None),
        P("section", None, None),
        P("section", None),
        P("section", None, None),
        P("section", None, None),
        P("section", None, None),
    )
    out_specs = (
        P("section", None, "seq", None),
        P("section", None, "seq", None),
        P("section", None, "seq", None),
        P("section", "seq"),
        P("section", "seq"),
        P("section", "seq", None),
        P("section", "seq", None),
        P("section", "seq", None),
        P("section", "seq"),
        P("section", "seq", None),
        P("section", "seq", None),
        P("section", "seq", None),
    )
    return jax.shard_map(on_device, mesh=mesh, in_specs=in_specs, out_specs=out_specs, check_vma=False)
```

```python
import functools
import math

import jax
import jax.numpy as jnp
from jax import lax
from jax.experimental import pallas as pl
from jax.experimental.pallas import tpu as pltpu
from jax.sharding import PartitionSpec as P

F32 = jnp.float32
BF16 = jnp.bfloat16
VMEM_BYTES = 56 * 1024 * 1024
LANES = 128


def gelu_and_slope(v):
    half_sq = jnp.exp(-0.5 * v * v)
    t = 1.0 / (1.0 + (0.3275911 * 0.7071067811865476) * jnp.abs(v))
    poly = t * (
        0.127414796 + t * (-0.142248368 + t * (0.7107068705 + t * (-0.7265760135 + t * 0.5307027145)))
    )
    tail = poly * half_sq
    cdf = jnp.where(v >= 0.0, 1.0 - tail, tail)
    return v * cdf, cdf + v * half_sq * 0.3989422804014327


def dot(left, right):
    return jnp.dot(left, right, preferred_element_type=F32)


def dot_t(left, right):
    return lax.dot_general(left, right, (((1,), (1,)), ((), ())), preferred_element_type=F32)


def dot_rows(left, right):
    return lax.dot_general(left, right, (((0,), (0,)), ((), ())), preferred_element_type=F32)


def fetch(own, mine, other, window, kept, sem):
    @pl.when(own)
    def _():
        pltpu.make_async_copy(mine.at[window], kept, sem).start()

    @pl.when(jnp.logical_not(own))
    def _():
        pltpu.make_async_copy(other.at[window], kept, sem).start()


def landed(mine, window, kept, sem):
    pltpu.make_async_copy(mine.at[window], kept, sem).wait()


def whole_of(ref):
    return tuple(pl.ds(0, size) for size in ref.shape)


def side_window(ref, axis, side, width):
    start = pl.multiple_of(side * width, LANES)
    return tuple(pl.ds(start, width) if d == axis else pl.ds(0, size) for d, size in enumerate(ref.shape))


def wide(values, width):
    return jnp.concatenate([values] * (width // LANES), axis=1)


def norm_parts(x):
    centre = x - jnp.mean(x, axis=-1, keepdims=True)
    spread = jnp.mean(centre * centre, axis=-1, keepdims=True)
    return centre, lax.rsqrt(spread + 1e-05)


def normed(x, gain_ref, bias_ref):
    centre, rstd = norm_parts(x)
    return (centre * rstd * gain_ref[...] + bias_ref[...]).astype(BF16)


def spread_rows(ref, rows):
    return jnp.broadcast_to(ref[...], (rows, ref.shape[1]))


def at(t, rows):
    return pl.ds(pl.multiple_of(t * rows, rows), rows)


def norm_kernel(layer, flags, x_ref, gain_ref, bias_ref, norm_ref, turned_ref):
    x = jnp.swapaxes(x_ref[...].astype(F32), 0, 1).reshape(norm_ref.shape)
    turned_ref[...] = x.astype(BF16)
    norm_ref[...] = normed(x, gain_ref, bias_ref)


def value_kernel(layer, flags, *refs):
    if layer == 0:
        norm_ref, *refs = refs
    else:
        x_ref, y_ref, z_ref, gain_ref, bias_ref, *refs = refs
    (wv_mine, wv_other, im_mine, im_other, retain_ref, inject_ref, through_ref, dead_ref, *refs) = refs
    if layer == 0:
        act_ref, slope_ref, drive_ref, carry_ref, wv, im, sems = refs
    else:
        act_ref, slope_ref, drive_ref, carry_ref, x1_ref, norm_ref, wv, im, sems = refs
    first = pl.program_id(0) == 0
    own = flags[layer] > 0

    @pl.when(first)
    def _():
        fetch(own, wv_mine, wv_other, whole_of(wv), wv, sems.at[0])
        fetch(own, im_mine, im_other, whole_of(im), im, sems.at[1])

    if layer == 0:
        norm = norm_ref[...]
    else:
        low = (x_ref[...].astype(F32) + (y_ref[...].astype(F32) + z_ref[...].astype(F32))).astype(BF16)
        x1_ref[...] = low
        norm = normed(low.astype(F32), gain_ref, bias_ref)
        norm_ref[...] = norm

    @pl.when(first)
    def _():
        landed(wv_mine, whole_of(wv), wv, sems.at[0])
        landed(im_mine, whole_of(im), im, sems.at[1])

    act, slope = gelu_and_slope(dot(norm, wv[...]))
    act = act.astype(BF16)
    act_ref[...] = act
    slope_ref[...] = slope.astype(BF16)
    drive_ref[...] = dot(act, im[...])
    rows = dead_ref.shape[1]
    width = retain_ref.shape[1]
    retain, inject = spread_rows(retain_ref, rows), spread_rows(inject_ref, rows)

    @pl.when(first)
    def _():
        carry_ref[:rows, :] = jnp.ones((rows, width), F32)
        carry_ref[rows:, :] = jnp.zeros((rows, width), F32)

    def step(t, state):
        through, end = state
        dead = wide(dead_ref[t], width)
        factor = wide(through_ref[t], width) * retain + dead
        return factor * through, factor * end + (1.0 - dead) * inject * drive_ref[at(t, rows), :]

    through, end = lax.fori_loop(
        0, dead_ref.shape[0], step, (carry_ref[:rows, :], carry_ref[rows:, :]), unroll=8
    )
    carry_ref[:rows, :] = through
    carry_ref[rows:, :] = end


def gate_kernel(part, layer, flags, norm_ref, wg_mine, wg_other, act_ref, slope_ref, wg, sems):
    width = wg.shape[1]
    start = pl.multiple_of(flags[2] * (wg_mine.shape[1] // 2) + part * width, LANES)
    window = (pl.ds(0, wg.shape[0]), pl.ds(start, width))

    @pl.when(pl.program_id(0) == 0)
    def _():
        fetch(flags[layer] > 0, wg_mine, wg_other, window, wg, sems.at[0])
        landed(wg_mine, window, wg, sems.at[0])

    act, slope = gelu_and_slope(dot(norm_ref[...], wg[...]))
    act_ref[...] = act.astype(BF16)
    slope_ref[...] = slope.astype(BF16)


def mix_kernel(parts, layer, flags, entry_ref, drive_ref, retain_ref, inject_ref, through_ref, dead_ref, *refs):
    acts, refs = refs[:parts], refs[parts:]
    (
        om_mine, om_other, wm_mine, wm_other, wd_mine, wd_other,
        low_ref, mixer_ref, mix_ref, hidden_ref, branch_ref, om, wm, wd, states, last, sems,
    ) = refs
    first = pl.program_id(0) == 0
    own = flags[layer] > 0
    half = wm.shape[1]
    wm_window = side_window(wm_mine, 1, flags[2], half)
    wd_window = side_window(wd_mine, 0, flags[2], half)

    @pl.when(first)
    def _():
        fetch(own, om_mine, om_other, whole_of(om), om, sems.at[0])
        fetch(own, wm_mine, wm_other, wm_window, wm, sems.at[1])
        fetch(own, wd_mine, wd_other, wd_window, wd, sems.at[2])
        last[...] = entry_ref[...]

    rows = dead_ref.shape[1]
    width = retain_ref.shape[1]
    retain, inject = spread_rows(retain_ref, rows), spread_rows(inject_ref, rows)

    def step(t, state):
        dead = wide(dead_ref[t], width)
        factor = wide(through_ref[t], width) * retain + dead
        state = factor * state + (1.0 - dead) * inject * drive_ref[at(t, rows), :]
        states[at(t, rows), :] = state
        return state

    last[...] = lax.fori_loop(0, dead_ref.shape[0], step, last[...], unroll=8)
    low = states[...].astype(BF16)
    low_ref[...] = low

    @pl.when(first)
    def _():
        landed(om_mine, whole_of(om), om, sems.at[0])
        landed(wm_mine, wm_window, wm, sems.at[1])
        landed(wd_mine, wd_window, wd, sems.at[2])

    mixer = dot(low, om[...]).astype(BF16)
    mixer_ref[...] = mixer
    step_width = half // parts
    branch = None
    for i, act_ref in enumerate(acts):
        here = slice(i * step_width, (i + 1) * step_width)
        value_mix = dot(mixer, wm[:, here])
        mix_ref[:, here] = value_mix.astype(BF16)
        hidden = (act_ref[...].astype(F32) * value_mix).astype(BF16)
        hidden_ref[:, here] = hidden
    branch_ref[...] = dot(hidden_ref[...], wd[...]).astype(BF16)


def middle_kernel(
    parts, layer, flags, entry_ref, drive_ref, grad_ref, retain_ref, inject_ref, through_ref, dead_ref, *refs
):
    acts, slopes, refs = refs[:parts], refs[parts : 2 * parts], refs[2 * parts :]
    (
        om_mine, om_other, wm_mine, wm_other, wd_mine, wd_other,
        low_ref, mixer_ref, hidden_ref, gate_low_ref, mix_low_ref, mixer_back_ref,
        om, wm, wd, states, last, sems,
    ) = refs
    first = pl.program_id(0) == 0
    own = flags[layer] > 0
    half = wm.shape[1]
    wm_window = side_window(wm_mine, 1, flags[2], half)
    wd_window = side_window(wd_mine, 0, flags[2], half)

    @pl.when(first)
    def _():
        fetch(own, om_mine, om_other, whole_of(om), om, sems.at[0])
        fetch(own, wm_mine, wm_other, wm_window, wm, sems.at[1])
        fetch(own, wd_mine, wd_other, wd_window, wd, sems.at[2])
        last[...] = entry_ref[...]

    rows = dead_ref.shape[1]
    width = retain_ref.shape[1]
    retain, inject = spread_rows(retain_ref, rows), spread_rows(inject_ref, rows)

    def step(t, state):
        dead = wide(dead_ref[t], width)
        factor = wide(through_ref[t], width) * retain + dead
        state = factor * state + (1.0 - dead) * inject * drive_ref[at(t, rows), :]
        states[at(t, rows), :] = state
        return state

    last[...] = lax.fori_loop(0, dead_ref.shape[0], step, last[...], unroll=8)
    low = states[...].astype(BF16)
    low_ref[...] = low

    @pl.when(first)
    def _():
        landed(om_mine, whole_of(om), om, sems.at[0])
        landed(wm_mine, wm_window, wm, sems.at[1])
        landed(wd_mine, wd_window, wd, sems.at[2])

    mixer = dot(low, om[...]).astype(BF16)
    mixer_ref[...] = mixer
    step_width = half // parts
    for i in range(parts):
        here = slice(i * step_width, (i + 1) * step_width)
        value_mix = dot(mixer, wm[:, here])
        act = acts[i][...].astype(F32)
        hidden_ref[:, here] = (act * value_mix).astype(BF16)
        d_hidden = dot_t(grad_ref[...], wd[here, :])
        gate_low_ref[:, here] = (slopes[i][...].astype(F32) * (d_hidden * value_mix)).astype(BF16)
        mix_low_ref[:, here] = (d_hidden * act).astype(BF16)
    mixer_back_ref[...] = dot_t(mix_low_ref[...], wm[...]).astype(BF16)


def branch_kernel(layer, flags, hidden_ref, wd_mine, wd_other, branch_ref, wd, sems):
    window = side_window(wd_mine, 0, flags[2], wd.shape[0])

    @pl.when(pl.program_id(0) == 0)
    def _():
        fetch(flags[layer] > 0, wd_mine, wd_other, window, wd, sems.at[0])
        landed(wd_mine, window, wd, sems.at[0])

    branch_ref[...] = dot(hidden_ref[...], wd[...]).astype(BF16)


def hidden_back_kernel(parts, layer, flags, grad_ref, mix_ref, *refs):
    acts, slopes, refs = refs[:parts], refs[parts : 2 * parts], refs[2 * parts :]
    wd_mine, wd_other, wm_mine, wm_other, gate_low_ref, mix_low_ref, mixer_ref, wd, wm, sems = refs
    own = flags[layer] > 0
    half = wm.shape[1]
    wm_window = side_window(wm_mine, 1, flags[2], half)
    wd_window = side_window(wd_mine, 0, flags[2], half)

    @pl.when(pl.program_id(0) == 0)
    def _():
        fetch(own, wd_mine, wd_other, wd_window, wd, sems.at[0])
        fetch(own, wm_mine, wm_other, wm_window, wm, sems.at[1])
        landed(wd_mine, wd_window, wd, sems.at[0])
        landed(wm_mine, wm_window, wm, sems.at[1])

    step_width = half // parts
    for i in range(parts):
        here = slice(i * step_width, (i + 1) * step_width)
        d_hidden = dot_t(grad_ref[...], wd[here, :])
        gate_low_ref[:, here] = (
            slopes[i][...].astype(F32) * (d_hidden * mix_ref[:, here].astype(F32))
        ).astype(BF16)
        mix_low_ref[:, here] = (d_hidden * acts[i][...].astype(F32)).astype(BF16)
    mixer_ref[...] = dot_t(mix_low_ref[...], wm[...]).astype(BF16)


def states_back_kernel(
    layer, flags, mixer_ref, mixer_other, retain_ref, through_ref, dead_ref, om_mine, om_other,
    mixer_low_ref, d_states_ref, carry_ref, om, sems,
):
    first = pl.program_id(0) == 0
    rows = dead_ref.shape[1]
    count = dead_ref.shape[0]
    width = retain_ref.shape[1]

    @pl.when(first)
    def _():
        fetch(flags[layer] > 0, om_mine, om_other, whole_of(om), om, sems.at[0])
        carry_ref[:rows, :] = jnp.ones((rows, width), F32)
        carry_ref[rows:, :] = jnp.zeros((rows, width), F32)
        landed(om_mine, whole_of(om), om, sems.at[0])

    low = (mixer_ref[...].astype(F32) + mixer_other[...].astype(F32)).astype(BF16)
    mixer_low_ref[...] = low
    d_states_ref[...] = dot_t(low, om[...])
    retain = spread_rows(retain_ref, rows)

    def step(i, state):
        t = count - 1 - i
        through, end = state
        factor = wide(through_ref[t], width) * retain + wide(dead_ref[t], width)
        return factor * through, factor * (end + d_states_ref[at(t, rows), :])

    through, end = lax.fori_loop(0, count, step, (carry_ref[:rows, :], carry_ref[rows:, :]), unroll=8)
    carry_ref[:rows, :] = through
    carry_ref[rows:, :] = end


def drive_back_kernel(
    layer, flags, back_ref, entry_ref, d_states_ref, states_ref, drive_ref, retain_ref, inject_ref, gain_ref,
    through_ref, dead_ref, slope_ref, im_mine, im_other,
    drive_low_ref, value_low_ref, rate_ref, im, states, d_drive, kept, sems,
):
    block = pl.program_id(0)
    rows = dead_ref.shape[1]
    count = dead_ref.shape[0]
    width = retain_ref.shape[1]

    @pl.when(block == 0)
    def _():
        fetch(flags[layer] > 0, im_mine, im_other, whole_of(im), im, sems.at[0])
        kept[0] = back_ref[...]
        kept[1] = jnp.zeros((rows, width), F32)
        kept[2] = jnp.zeros((rows, width), F32)
        kept[3] = jnp.zeros((rows, width), F32)
        landed(im_mine, whole_of(im), im, sems.at[0])

    retain, inject = spread_rows(retain_ref, rows), spread_rows(inject_ref, rows)
    states[...] = states_ref[...].astype(F32)

    def step(i, state):
        carried, flow, decay_sum, inject_sum = state
        t = count - 1 - i
        here = at(t, rows)
        dead = wide(dead_ref[t], width)
        lam = d_states_ref[here, :] + carried
        decay_sum = decay_sum + flow * states[here, :]
        alive = (1.0 - dead) * lam
        d_drive[here, :] = alive * inject
        inject_sum = inject_sum + alive * drive_ref[here, :]
        flow = wide(through_ref[t], width) * lam
        return flow * retain + dead * lam, flow, decay_sum, inject_sum

    carried, flow, decay_sum, inject_sum = lax.fori_loop(
        0, count, step, (kept[0], kept[1], kept[2], kept[3]), unroll=8
    )
    kept[0] = carried
    kept[1] = flow
    kept[2] = decay_sum
    kept[3] = inject_sum

    @pl.when(block == pl.num_programs(0) - 1)
    def _():
        rate_ref[...] = jnp.sum(
            gain_ref[...] * inject_sum - retain * (decay_sum + flow * entry_ref[...]), axis=0, keepdims=True
        )

    low = d_drive[...].astype(BF16)
    drive_low_ref[...] = low
    value_low_ref[...] = (slope_ref[...].astype(F32) * dot_t(low, im[...])).astype(BF16)


def gate_back_kernel(layer, flags, gate_low_ref, wg_mine, wg_other, d_norm_ref, wg, sems):
    window = side_window(wg_mine, 1, flags[2], wg.shape[1])

    @pl.when(pl.program_id(0) == 0)
    def _():
        fetch(flags[layer] > 0, wg_mine, wg_other, window, wg, sems.at[0])
        landed(wg_mine, window, wg, sems.at[0])

    d_norm_ref[...] = dot_t(gate_low_ref[...], wg[...]).astype(BF16)


def norm_back_kernel(
    layer, flags, grad_ref, d_norm_ref, d_norm_other, value_low_ref, x_ref, gain_ref, wv_mine, wv_other,
    d_x_ref, d_x_low_ref, vector_ref, wv, sems,
):
    @pl.when(pl.program_id(0) == 0)
    def _():
        fetch(flags[layer] > 0, wv_mine, wv_other, whole_of(wv), wv, sems.at[0])
        vector_ref[...] = jnp.zeros_like(vector_ref)
        landed(wv_mine, whole_of(wv), wv, sems.at[0])

    d_norm = (d_norm_ref[...].astype(F32) + d_norm_other[...].astype(F32)) + dot_t(value_low_ref[...], wv[...])
    centre, rstd = norm_parts(x_ref[...].astype(F32))
    xhat = centre * rstd
    vector_ref[0:1, :] += jnp.sum(d_norm * xhat, axis=0, keepdims=True)
    vector_ref[1:2, :] += jnp.sum(d_norm, axis=0, keepdims=True)
    scaled = d_norm * gain_ref[...]
    first = jnp.mean(scaled, axis=-1, keepdims=True)
    second = jnp.mean(scaled * xhat, axis=-1, keepdims=True)
    d_x = grad_ref[...].astype(F32) + (scaled - first - xhat * second) * rstd
    d_x_ref[...] = d_x
    d_x_low_ref[...] = d_x.astype(BF16)


def shape(dims, dtype):
    return jax.ShapeDtypeStruct(dims, dtype)


def run(kernel, flags, grid, operands, outs, scratch, flops=0):
    arrays = [far(array) if array.size >= 65536 else array for array, _ in operands]
    held = 6 * 1024 * 1024
    for array, spec in operands + outs:
        if spec.block_shape is not None:
            held += 2 * math.prod(spec.block_shape) * array.dtype.itemsize
    for item in scratch:
        if item.dtype in (F32, BF16):
            held += math.prod(item.shape) * item.dtype.itemsize
    return pl.pallas_call(
        kernel,
        out_shape=[struct for struct, _ in outs],
        grid_spec=pltpu.PrefetchScalarGridSpec(
            num_scalar_prefetch=1,
            grid=grid,
            in_specs=[spec for _, spec in operands],
            out_specs=[spec for _, spec in outs],
            scratch_shapes=scratch,
        ),
        cost_estimate=pl.CostEstimate(flops=0, bytes_accessed=0, transcendentals=0),
        compiler_params=pltpu.CompilerParams(
            vmem_limit_bytes=held, dimension_semantics=("arbitrary",) * len(grid)
        ),
    )(flags, *arrays)


def far(array):
    return pltpu.with_memory_space_constraint(array, pltpu.HBM)


def whole(dims):
    return pl.BlockSpec(dims, lambda *_: (0,) * len(dims))


class Reduction:
    def __init__(self, arrays, bits, mine):
        self.left = tuple(sorted(bits, reverse=True))
        self.terms = [(tuple(arrays), self.left, None)]
        self.fixed = {}
        self.mine = mine
        self.height = sum(array.shape[-2] for array in arrays)

    def part(self, fixed):
        left = [bit for bit in self.left if bit not in fixed]
        total = None
        for arrays, bits, at_row in self.terms:
            pieces = []
            for array in arrays:
                block = array.shape[len(bits) :]
                starts = [fixed.get(bit, 0) for bit in bits] + [at_row or 0, 0]
                if at_row is not None:
                    block = (self.height, *block[1:])
                sizes = [1 if bit in fixed else 2 for bit in bits] + list(block)
                pieces.append(lax.dynamic_slice(array, starts, sizes).reshape((2,) * len(left) + tuple(block)))
            term = pieces[0] if len(pieces) == 1 else jnp.concatenate(pieces, axis=-2)
            term = term.astype(F32)
            total = term if total is None else total + term
        return total

    def message(self, bit):
        away = dict(self.fixed)
        away[bit] = 1 - self.mine[bit]
        return self.part(away).astype(BF16)

    def step(self, bit):
        self.send(bit, self.message(bit))

    def send(self, bit, sent):
        count = lax.axis_size("seq")
        self.take(bit, lax.ppermute(sent, "seq", [(i, i ^ (1 << bit)) for i in range(count)]))

    def take(self, bit, came, at_row=0):
        self.fixed[bit] = self.mine[bit]
        self.terms.append(((came,), tuple(b for b in self.left if b not in self.fixed), at_row))

    def result(self):
        return self.part(self.fixed)


def arrived(reductions):
    return [part.terms[-1][0] for part in reductions]


def put_back(reductions, arrays):
    for part, array in zip(reductions, arrays):
        part.terms[-1] = (array, *part.terms[-1][1:])


def awaited(token, *reductions):
    token, came = lax.optimization_barrier((token, arrived(reductions)))
    put_back(reductions, came)
    return token


def carried(pieces, mine, backward, anchor=None, fillers=(), sends=(), waits=()):
    rows = pieces.shape[0] // 2
    count = lax.axis_size("seq")
    through, end = pieces[:rows], pieces[rows:]
    before_through, before_end = jnp.ones_like(through), jnp.zeros_like(end)
    filled = []
    for bit in range(len(mine)):
        message = jnp.concatenate([through, end], axis=0)
        if bit < len(fillers):
            message, anchor, filled = lax.optimization_barrier((message, anchor, filled))
        if bit < len(waits) and waits[bit]:
            message = awaited(message, *waits[bit])
        came = lax.ppermute(message, "seq", [(i, i ^ (1 << bit)) for i in range(count)])
        if bit < len(sends) and sends[bit] is not None:
            sends[bit](filled)
        if bit < len(fillers):
            filled = filled + [fillers[bit](anchor, filled)]
            came, filled = lax.optimization_barrier((came, filled))
        far_through, far_end = came[:rows], came[rows:]
        first = mine[bit] == (0 if backward else 1)
        before_end = jnp.where(first, before_through * far_end + before_end, before_end)
        before_through = jnp.where(first, before_through * far_through, before_through)
        end = jnp.where(first, through * far_end + end, far_through * end + far_end)
        through = through * far_through
    for filler in fillers[len(mine) :]:
        filled = filled + [filler(anchor, filled)]
    return before_through, before_end, filled


def swap(array):
    return lax.ppermute(array, "section", [(0, 1), (1, 0)])


def on_device(
    inputs, cotangent, lengths, keep, init_states, ln_gain, ln_bias, w_gate, w_value, in_map, rates, out_map,
    w_mix, w_down,
):
    rows, count, width = inputs.shape
    tokens = rows * count
    gate_width = w_gate.shape[2]
    half = gate_width // 2
    value_width = w_value.shape[2]
    state_width = in_map.shape[2]
    section = lax.axis_index("section")
    piece = lax.axis_index("seq")
    pieces = lax.axis_size("seq")
    bits = pieces.bit_length() - 1
    mine = [(piece >> bit) & 1 for bit in range(bits)]
    block = 256 if tokens % 256 == 0 else tokens
    grid = (tokens // block,)
    parts = 2

    any_spec = pl.BlockSpec(memory_space=pl.ANY)

    def pair(mine, other):
        return [(far(mine), any_spec), (far(other), any_spec)]

    my_vectors = jnp.concatenate([ln_gain[0], ln_bias[0], rates[0], init_states[0].reshape(-1)])
    vectors = swap(my_vectors)
    wv_other, im_other = swap(w_value[0]), swap(in_map[0])
    wv, im = pair(w_value[0], wv_other), pair(in_map[0], im_other)
    wg_mine, inputs, _, _ = lax.optimization_barrier((w_gate[0], inputs, wv_other, im_other))
    wg = pair(wg_mine, swap(wg_mine))
    flags = jnp.stack([(section == 0).astype(jnp.int32), (section == 1).astype(jnp.int32), section.astype(jnp.int32)])

    grad_top = cotangent.transpose(1, 0, 2).reshape(tokens, width)

    positions = piece * count + jnp.arange(count, dtype=jnp.int32)
    first_len, second_len = lengths[:, 0][None, :], lengths[:, 1][None, :]
    live = positions[:, None] < first_len + second_len
    reset = (positions[:, None] == first_len) & (second_len > 0)
    through = jnp.where(live & jnp.logical_not(reset), keep.T, 0.0)
    dead = jnp.where(live, 0.0, 1.0).astype(F32)
    through = jnp.broadcast_to(through[:, :, None], (count, rows, LANES))
    dead = jnp.broadcast_to(dead[:, :, None], (count, rows, LANES))
    mask_dims = (block // rows, rows, LANES)
    end_block = grid[0] - 1
    mask_spec = pl.BlockSpec(mask_dims, lambda i, f: (i, 0, 0))
    back_mask_spec = pl.BlockSpec(mask_dims, lambda i, f: (end_block - i, 0, 0))
    masks = [(through, mask_spec), (dead, mask_spec)]
    back_masks = [(through, back_mask_spec), (dead, back_mask_spec)]

    def by_rows(cols):
        return pl.BlockSpec((block, cols), lambda i, f: (i, 0))

    def by_rows_back(cols):
        return pl.BlockSpec((block, cols), lambda i, f: (end_block - i, 0))

    def out(cols, dtype=BF16, back=False):
        struct = pltpu.HBM((tokens, cols), dtype)
        return (struct, by_rows_back(cols) if back else by_rows(cols))

    def sems(n):
        return pltpu.SemaphoreType.DMA((n,))

    carry_dims = (2 * rows, state_width)
    carry_out = (shape(carry_dims, F32), whole(carry_dims))
    row_state = whole((rows, state_width))
    wv_dims, im_dims, om_dims = (width, value_width), (value_width, state_width), (state_width, value_width)
    wg_dims, wm_dims, wd_dims = (width, half), (value_width, half), (half, width)

    layers = []
    for layer in range(2):
        chosen = jnp.where(section == layer, my_vectors, vectors)
        gain, bias, rate = (
            chosen[:width][None],
            chosen[width : 2 * width][None],
            chosen[2 * width : 2 * width + state_width][None],
        )
        start = chosen[2 * width + state_width :].reshape(rows, state_width)
        inject = jnp.sqrt(-jnp.expm1(-2.0 * rate))
        one_width, one_state = whole((1, width)), whole((1, state_width))
        layers.append(
            dict(
                gain=(gain, one_width),
                bias=(bias, one_width),
                retain=(jnp.exp(-rate), one_state),
                inject=(inject, one_state),
                rate_gain=(jnp.exp(-2.0 * rate) / inject, one_state),
                start=start,
            )
        )

    saved = []
    ends = []
    branch = None
    for layer in range(2):
        now = layers[layer]
        outs = [out(value_width), out(value_width), out(state_width, F32), carry_out]
        if layer == 0:
            by_positions = pl.BlockSpec((rows, block // rows, width), lambda i, f: (0, i, 0))
            norm, x0 = run(
                functools.partial(norm_kernel, layer),
                flags,
                grid,
                [(far(inputs), by_positions), now["gain"], now["bias"]],
                [out(width), out(width)],
                [],
            )
            x = x0
            sources = [(norm, by_rows(width))]
        else:
            sources = [
                (far(x0), by_rows(width)), (far(branch), by_rows(width)), (far(swap(branch)), by_rows(width)),
                now["gain"], now["bias"],
            ]
            outs += [out(width), out(width)]
        value_act, value_slope, drive, pieces_map, *more = run(
            functools.partial(value_kernel, layer),
            flags,
            grid,
            sources + wv + im + [now["retain"], now["inject"]] + masks,
            outs,
            [pltpu.VMEM(wv_dims, BF16), pltpu.VMEM(im_dims, BF16), sems(2)],
            flops=2 * tokens * (width * value_width + value_width * state_width),
        )
        if more:
            x, norm = more
        if layer == 0:
            pieces_map, *rest = lax.optimization_barrier((pieces_map, out_map[0], w_mix[0], w_down[0]))
            om, wm, wd = (pair(array, swap(array)) for array in rest)

        def gate_part(norm, filled, part, layer=layer):
            cols = half // parts
            return run(
                functools.partial(gate_kernel, part, layer),
                flags,
                grid,
                [(norm, by_rows(width))] + wg,
                [out(cols)] * 2,
                [pltpu.VMEM((width, cols), BF16), sems(1)],
                flops=2 * tokens * width * cols,
            )

        before_through, before_end, gates = carried(
            pieces_map, mine, False, norm, [functools.partial(gate_part, part=part) for part in range(parts)]
        )
        gate_act = [act for act, _ in gates]
        gate_slope = [slope for _, slope in gates]
        entry = before_through * now["start"] + before_end
        ends.append(pieces_map[:rows] * entry + pieces_map[rows:])
        if layer == 0:
            states_low, mixer, value_mix, hidden, branch = run(
                functools.partial(mix_kernel, parts, layer),
                flags,
                grid,
                [(entry, row_state), (drive, by_rows(state_width)), now["retain"], now["inject"]]
                + masks
                + [(act, by_rows(half // parts)) for act in gate_act]
                + om
                + wm
                + wd,
                [out(cols) for cols in (state_width, value_width, half, half, width)],
                [
                    pltpu.VMEM(om_dims, BF16),
                    pltpu.VMEM(wm_dims, BF16),
                    pltpu.VMEM(wd_dims, BF16),
                    pltpu.VMEM((block, state_width), F32),
                    pltpu.VMEM((rows, state_width), F32),
                    sems(3),
                ],
                flops=2 * tokens * (state_width * value_width + value_width * half + half * width),
            )
        else:
            value_mix = None
            states_low, mixer, hidden, gate_low, mix_low, mixer_part = run(
                functools.partial(middle_kernel, parts, layer),
                flags,
                grid,
                [
                    (entry, row_state), (drive, by_rows(state_width)), (far(grad_top), by_rows(width)),
                    now["retain"], now["inject"],
                ]
                + masks
                + [(array, by_rows(half // parts)) for array in gate_act + gate_slope]
                + om
                + wm
                + wd,
                [
                    out(state_width), out(value_width), out(half), out(half), out(half),
                    out(value_width),
                ],
                [
                    pltpu.VMEM(om_dims, BF16),
                    pltpu.VMEM(wm_dims, BF16),
                    pltpu.VMEM(wd_dims, BF16),
                    pltpu.VMEM((block, state_width), F32),
                    pltpu.VMEM((rows, state_width), F32),
                    sems(3),
                ],
                flops=2 * tokens * (state_width * value_width + 2 * value_width * half + 2 * half * width),
            )
        saved.append(
            dict(
                x=x, norm=norm, value_act=value_act, value_slope=value_slope, drive=drive, gate_act=gate_act,
                gate_slope=gate_slope, entry=entry, states_low=states_low, mixer=mixer,
                value_mix=value_mix, hidden=hidden,
            )
        )
    x1 = saved[1]["x"]

    def gate_norm_part(layer, gate_low):
        return run(
            functools.partial(gate_back_kernel, layer),
            flags,
            grid,
            [(gate_low, by_rows(half))] + wg,
            [out(width)],
            [pltpu.VMEM(wg_dims, BF16), sems(1)],
            flops=2 * tokens * half * width,
        )[0]

    def hidden_back(layer, grad):
        kept = saved[layer]
        return run(
            functools.partial(hidden_back_kernel, parts, layer),
            flags,
            grid,
            [(grad, by_rows(width)), (far(kept["value_mix"]), by_rows(half))]
            + [(far(array), by_rows(half // parts)) for array in kept["gate_act"] + kept["gate_slope"]]
            + wd
            + wm,
            [out(half), out(half), out(value_width)],
            [pltpu.VMEM(wd_dims, BF16), pltpu.VMEM(wm_dims, BF16), sems(2)],
            flops=2 * tokens * half * (width + value_width),
        )

    def states_back(layer, mixer_part, mixer_other):
        return run(
            functools.partial(states_back_kernel, layer),
            flags,
            grid,
            [
                (far(mixer_part), by_rows_back(value_width)),
                (far(mixer_other), by_rows_back(value_width)),
                layers[layer]["retain"],
            ]
            + back_masks
            + om,
            [out(value_width, back=True), out(state_width, F32, back=True), carry_out],
            [pltpu.VMEM(om_dims, BF16), sems(1)],
            flops=2 * tokens * state_width * value_width,
        )

    def drive_back(layer, back, d_states):
        now, kept = layers[layer], saved[layer]
        return run(
            functools.partial(drive_back_kernel, layer),
            flags,
            grid,
            [
                (back, row_state),
                (kept["entry"], row_state),
                (d_states, by_rows_back(state_width)),
                (far(kept["states_low"]), by_rows_back(state_width)),
                (far(kept["drive"]), by_rows_back(state_width)),
                now["retain"],
                now["inject"],
                now["rate_gain"],
            ]
            + back_masks
            + [(far(kept["value_slope"]), by_rows_back(value_width))]
            + im,
            [
                out(state_width, back=True),
                out(value_width, back=True),
                (shape((1, state_width), F32), whole((1, state_width))),
            ],
            [
                pltpu.VMEM(im_dims, BF16),
                pltpu.VMEM((block, state_width), F32),
                pltpu.VMEM((block, state_width), F32),
                pltpu.VMEM((4, rows, state_width), F32),
                sems(1),
            ],
            flops=2 * tokens * state_width * value_width,
        )

    def norm_back(layer, grad, d_norm_part, d_norm_other, value_low):
        return run(
            functools.partial(norm_back_kernel, layer),
            flags,
            grid,
            [
                (far(grad), by_rows(width)),
                (far(d_norm_part), by_rows(width)),
                (far(d_norm_other), by_rows(width)),
                (value_low, by_rows(value_width)),
                (far(saved[layer]["x"]), by_rows(width)),
                layers[layer]["gain"],
            ]
            + wv,
            [
                out(width, F32),
                out(width),
                (shape((8, width), F32), whole((8, width))),
            ],
            [pltpu.VMEM(wv_dims, BF16), sems(1)],
            flops=2 * tokens * value_width * width,
        )

    def reductions(d_down, d_gate, d_mix):
        return (
            Reduction([d_down.reshape((2,) * (bits - 1) + (-1, width))], range(bits - 1), mine),
            Reduction([d_gate.reshape((2,) * bits + (-1, half))], range(bits), mine),
            Reduction([d_mix.reshape((2,) * bits + (-1, half))], range(bits), mine),
        )

    cols = value_width // 2

    def sides(layer, value_low, drive_low, mixer_low):
        def my_side(array):
            return lax.dynamic_slice(array, (0, section * cols), (tokens, cols))

        return [
            dot_rows(left, my_side(right)).astype(BF16)
            for left, right in (
                (saved[layer]["norm"], value_low),
                (saved[layer]["value_act"], drive_low),
                (saved[layer]["states_low"], mixer_low),
            )
        ]

    def vector_of(norm_vectors, grad_rate):
        vector = jnp.concatenate(
            [
                norm_vectors[0].reshape(pieces, -1),
                norm_vectors[1].reshape(pieces, -1),
                grad_rate.reshape(pieces, -1),
            ],
            axis=1,
        ).astype(BF16)
        return jnp.pad(vector[:, None, :], ((0, 0), (0, 15), (0, cols - vector.shape[1])))

    def small_of(side_grads, *vectors_):
        arrays = [array.reshape(pieces, -1, cols) for array in side_grads] + [vector_of(*v) for v in vectors_]
        (joint,) = tied(jnp.concatenate(arrays, axis=1))
        return joint.reshape((2,) * bits + joint.shape[1:])

    def tied(*arrays):
        return lax.optimization_barrier(arrays)

    def joint_message(reductions, bit):
        return jnp.concatenate([part.message(bit) for part in reductions], axis=-2)

    def joint_send(reductions, bit, message):
        came = lax.ppermute(message, "seq", [(i, i ^ (1 << bit)) for i in range(pieces)])
        at_row = 0
        for part in reductions:
            part.take(bit, came, at_row)
            at_row += part.height

    def joint_step(reductions, bit):
        joint_send(reductions, bit, joint_message(reductions, bit))

    def final_down(layer, part):
        top = pieces // 2
        sent = part.astype(BF16)
        mate = 1 - layer
        across = [
            pair
            for low in range(top)
            for pair in (
                (layer * pieces + mate * top + low, layer * pieces + layer * top + low),
                (mate * pieces + layer * top + low, layer * pieces + mate * top + low),
            )
        ]
        beside = [(mate * pieces + mate * top + low, layer * pieces + mate * top + low) for low in range(top)]
        came = lax.ppermute(sent, ("section", "seq"), across).astype(F32)
        came = came + lax.ppermute(sent, ("section", "seq"), beside).astype(F32)
        return jnp.where(mine[bits - 1] == layer, part, 0.0) + came

    share = value_width // pieces
    order = list(range(bits - 1))
    down_order = order
    gate_order = order[1:2] + order[:1] + order[2:]
    mix_order = order[-1:] + order[:-1]
    small_order = [*mix_order[:1], *order[1:-1], *order[:1], bits - 1] if len(order) > 1 else [*order, bits - 1]
    orders = (down_order, gate_order, mix_order)

    def back_carry(layer, back_map, d_down, grads, with_norm):
        parts_ = [Reduction([d_down.reshape((2,) * (bits - 1) + (-1, width))], range(bits - 1), mine)]

        def gate_filler(a, filled):
            return dot_rows(a[0], a[1]).astype(BF16), parts_[0].message(down_order[0])

        def norm_filler(a, filled):
            gate = Reduction([filled[0][0].reshape((2,) * bits + (-1, half))], range(bits), mine)
            parts_.append(gate)
            message = gate.message(gate_order[0])
            return (message, gate_norm_part(layer, a[1])) if with_norm else (message,)

        def mix_filler(a, filled):
            mix = Reduction(
                [dot_rows(a[2], a[3]).astype(BF16).reshape((2,) * bits + (-1, half))], range(bits), mine
            )
            parts_.append(mix)
            return mix.message(mix_order[0])

        sends = [
            None,
            lambda filled: parts_[0].send(down_order[0], filled[0][1]),
            lambda filled: parts_[1].send(gate_order[0], filled[1][0]),
        ]
        _, back, filled = carried(back_map, mine, True, grads, [gate_filler, norm_filler, mix_filler], sends)
        back, message = tied(back, filled[2])
        parts_[2].send(mix_order[0], message)
        return back, parts_, filled[1][-1]

    kept = saved[1]
    mixer_other = swap(mixer_part)
    d_down = dot_rows(kept["hidden"], grad_top).astype(BF16)
    mixer_low, d_states, back_map = states_back(1, mixer_part, mixer_other)
    back_map, d_down = tied(back_map, d_down)
    back, ones, d_norm_part = back_carry(
        1, back_map, d_down, (kept["norm"], gate_low, kept["mixer"], mix_low), True
    )
    down_one, gate_one, mix_one = ones
    d_norm_other = swap(d_norm_part)
    drive_low, value_low, grad_rate = drive_back(1, back, d_states)
    value_low = awaited(value_low, down_one)
    value_low, message = tied(value_low, down_one.message(down_order[1]))
    down_one.send(down_order[1], message)
    d_x1, grad, norm_vectors = norm_back(1, grad_top, d_norm_part, d_norm_other, value_low)
    small_one = small_of(sides(1, value_low, drive_low, mixer_low), (norm_vectors, grad_rate))
    grad, small_one = awaited((grad, small_one), gate_one, mix_one)
    grad, small_one, message = tied(grad, small_one, joint_message(ones[1:], order[0]))
    small_one = Reduction([small_one], range(bits), mine)
    joint_send(ones[1:], order[0], message)
    small_one.step(small_order[0])

    kept = saved[0]
    gate_low, mix_low, mixer_part = hidden_back(0, grad)
    mixer_other = swap(mixer_part)
    d_norm_part = gate_norm_part(0, gate_low)
    grad, mix_low, gate_low, d_norm_part = awaited(
        (grad, mix_low, gate_low, d_norm_part), down_one, gate_one, mix_one, small_one
    )
    d_norm_other = swap(d_norm_part)
    for place in range(2, len(order)):
        for part, order_ in zip(ones, orders):
            part.step(order_[place])
    d_down = dot_rows(kept["hidden"], grad).astype(BF16)
    mixer_part, mixer_other, d_down, d_norm_other = tied(mixer_part, mixer_other, d_down, d_norm_other)
    mixer_low, d_states, back_map = states_back(0, mixer_part, mixer_other)
    back_map, d_down = awaited((back_map, d_down), *ones)
    back, zeros, _ = back_carry(0, back_map, d_down, (kept["norm"], gate_low, kept["mixer"], mix_low), False)
    down_zero, gate_zero, mix_zero = zeros
    drive_low, value_low, grad_rate = drive_back(0, back, d_states)
    d_x0, _, norm_vectors = norm_back(0, grad, d_norm_part, d_norm_other, value_low)
    token = awaited((norm_vectors, value_low, drive_low), down_zero, gate_zero, mix_zero)
    joint_step(zeros[1:], order[0])
    down_zero.step(down_order[1])
    joint_step(ones[1:], bits - 1)
    grad_down_one = final_down(1, down_one.result())
    norm_vectors, value_low, drive_low = token
    small_zero = Reduction([small_of(sides(0, value_low, drive_low, mixer_low))], range(bits), mine)
    small_zero.step(small_order[0])
    hidden_one, _ = tied(saved[1]["hidden"], norm_vectors)
    (branch,) = run(
        functools.partial(branch_kernel, 1),
        flags,
        grid,
        [(hidden_one, by_rows(half))] + wd,
        [out(width)],
        [pltpu.VMEM(wd_dims, BF16), sems(1)],
    )
    branch = awaited(branch, down_zero)
    for place in range(2, len(order)):
        down_zero.step(down_order[place])
    (token, branch, x1, d_x0, d_x1, grad_down_one) = awaited(
        (norm_vectors, branch, x1, d_x0, d_x1, grad_down_one), *zeros[1:], *ones[1:], small_zero
    )
    for place in range(2, len(order)):
        for part, order_ in zip(zeros[1:], orders[1:]):
            part.step(order_[place])
    smalls = (small_one, small_zero)
    joint_step(smalls, small_order[-2])
    vector_zero = vector_of(token, grad_rate)
    vector_zero = Reduction([vector_zero.reshape((2,) * bits + vector_zero.shape[1:])], range(bits), mine)
    vector_zero.step(0)
    branch_other = swap(branch)
    token = awaited(token, *zeros, *smalls, vector_zero)
    joint_step(zeros[1:], bits - 1)
    grad_down_zero = final_down(0, down_zero.result())
    for place in range(1, len(order) - 1):
        joint_step(smalls, small_order[place])
    for bit in range(1, bits - 1):
        vector_zero.step(bit)
    token = awaited(token, *smalls, vector_zero)
    joint_step(smalls, bits - 1)
    vector_zero.step(bits - 1)
    reduced = [
        [grad_down_zero, gate_zero.result(), mix_zero.result()],
        [grad_down_one, gate_one.result(), mix_one.result(), small_one.result()],
    ]
    reduced[0].append(jnp.concatenate([small_zero.result(), vector_zero.result()], axis=0))
    d_xs = [d_x0, d_x1]

    second_out = (x1.astype(F32) + (branch.astype(F32) + branch_other.astype(F32))).astype(BF16)
    block_out = jnp.where(section == 0, x1, second_out)

    keep_own = [jnp.where(section == 0, a, b) for a, b in zip(reduced[0], reduced[1])]
    give = [jnp.where(section == 0, b, a).astype(BF16) for a, b in zip(reduced[0][1:], reduced[1][1:])]
    taken_wide = swap(jnp.concatenate(give[:2], axis=0))
    taken_small = swap(give[2]).astype(F32)
    cut = give[0].shape[0]
    taken = [taken_wide[:cut].astype(F32), taken_wide[cut:].astype(F32)]

    def joined(own, other):
        return jnp.where(
            section == 0, jnp.concatenate([own, other], axis=-1), jnp.concatenate([other, own], axis=-1)
        )

    grad_down = keep_own[0]
    grad_gate = joined(keep_own[1], taken[0])
    grad_mix = joined(keep_own[2], taken[1])
    small = joined(keep_own[3], taken_small)
    part = width // pieces
    grad_value, grad_input, grad_output = small[:part], small[part : part + share], small[part + share : part + 2 * share]
    vector = keep_own[3][part + 2 * share]
    grad_gain, grad_bias = vector[:part], vector[part : 2 * part]
    grad_rates = vector[2 * part : 2 * part + state_width // pieces]
    grad_in = jnp.where(section == 0, d_xs[0], d_xs[1])
    end_states = jnp.where(section == 0, ends[0], ends[1])

    def by_row(array):
        return array.reshape(count, rows, width).transpose(1, 0, 2)[None]

    return (
        by_row(block_out),
        by_row(grad_in),
        end_states[None, :, None, :],
        grad_gain[None],
        grad_bias[None],
        grad_gate[None],
        grad_value[None],
        grad_input[None],
        grad_rates[None],
        grad_output[None],
        grad_mix[None],
        grad_down[None],
    )


def solution(mesh):
    in_specs = (
        P(None, "seq", None),
        P(None, "seq", None),
        P(),
        P(None, "seq"),
        P("section", None, None),
        P("section", None),
        P("section", None),
        P("section", None, None),
        P("section", None, None),
        P("section", None, None),
        P("section", None),
        P("section", None, None),
        P("section", None, None),
        P("section", None, None),
    )
    out_specs = (
        P("section", None, "seq", None),
        P("section", None, "seq", None),
        P("section", None, "seq", None),
        P("section", "seq"),
        P("section", "seq"),
        P("section", "seq", None),
        P("section", "seq", None),
        P("section", "seq", None),
        P("section", "seq"),
        P("section", "seq", None),
        P("section", "seq", None),
        P("section", "seq", None),
    )
    return jax.shard_map(on_device, mesh=mesh, in_specs=in_specs, out_specs=out_specs, check_vma=False)
```

```python
import functools
import math

import jax
import jax.numpy as jnp
from jax import lax
from jax.experimental import pallas as pl
from jax.experimental.pallas import tpu as pltpu
from jax.sharding import PartitionSpec as P

F32 = jnp.float32
BF16 = jnp.bfloat16
VMEM_BYTES = 56 * 1024 * 1024
LANES = 128


def gelu_and_slope(v):
    half_sq = jnp.exp(-0.5 * v * v)
    t = 1.0 / (1.0 + (0.3275911 * 0.7071067811865476) * jnp.abs(v))
    poly = t * (
        0.127414796 + t * (-0.142248368 + t * (0.7107068705 + t * (-0.7265760135 + t * 0.5307027145)))
    )
    tail = poly * half_sq
    cdf = jnp.where(v >= 0.0, 1.0 - tail, tail)
    return v * cdf, cdf + v * half_sq * 0.3989422804014327


def dot(left, right):
    return jnp.dot(left, right, preferred_element_type=F32)


def dot_t(left, right):
    return lax.dot_general(left, right, (((1,), (1,)), ((), ())), preferred_element_type=F32)


def dot_rows(left, right):
    return lax.dot_general(left, right, (((0,), (0,)), ((), ())), preferred_element_type=F32)


def fetch(own, mine, other, window, kept, sem):
    @pl.when(own)
    def _():
        pltpu.make_async_copy(mine.at[window], kept, sem).start()

    @pl.when(jnp.logical_not(own))
    def _():
        pltpu.make_async_copy(other.at[window], kept, sem).start()


def landed(mine, window, kept, sem):
    pltpu.make_async_copy(mine.at[window], kept, sem).wait()


def whole_of(ref):
    return tuple(pl.ds(0, size) for size in ref.shape)


def side_window(ref, axis, side, width):
    start = pl.multiple_of(side * width, LANES)
    return tuple(pl.ds(start, width) if d == axis else pl.ds(0, size) for d, size in enumerate(ref.shape))


def wide(values, width):
    return jnp.concatenate([values] * (width // LANES), axis=1)


def norm_parts(x):
    centre = x - jnp.mean(x, axis=-1, keepdims=True)
    spread = jnp.mean(centre * centre, axis=-1, keepdims=True)
    return centre, lax.rsqrt(spread + 1e-05)


def normed(x, gain_ref, bias_ref):
    centre, rstd = norm_parts(x)
    return (centre * rstd * gain_ref[...] + bias_ref[...]).astype(BF16)


def spread_rows(ref, rows):
    return jnp.broadcast_to(ref[...], (rows, ref.shape[1]))


def at(t, rows):
    return pl.ds(pl.multiple_of(t * rows, rows), rows)


def norm_kernel(layer, flags, x_ref, gain_ref, bias_ref, norm_ref, turned_ref):
    x = jnp.swapaxes(x_ref[...].astype(F32), 0, 1).reshape(norm_ref.shape)
    turned_ref[...] = x.astype(BF16)
    norm_ref[...] = normed(x, gain_ref, bias_ref)


def value_kernel(layer, flags, *refs):
    if layer == 0:
        norm_ref, *refs = refs
    else:
        x_ref, y_ref, z_ref, gain_ref, bias_ref, *refs = refs
    (wv_mine, wv_other, im_mine, im_other, retain_ref, inject_ref, through_ref, dead_ref, *refs) = refs
    if layer == 0:
        act_ref, slope_ref, drive_ref, carry_ref, wv, im, sems = refs
    else:
        act_ref, slope_ref, drive_ref, carry_ref, x1_ref, norm_ref, wv, im, sems = refs
    first = pl.program_id(0) == 0
    own = flags[layer] > 0

    @pl.when(first)
    def _():
        fetch(own, wv_mine, wv_other, whole_of(wv), wv, sems.at[0])
        fetch(own, im_mine, im_other, whole_of(im), im, sems.at[1])

    if layer == 0:
        norm = norm_ref[...]
    else:
        low = (x_ref[...].astype(F32) + (y_ref[...].astype(F32) + z_ref[...].astype(F32))).astype(BF16)
        x1_ref[...] = low
        norm = normed(low.astype(F32), gain_ref, bias_ref)
        norm_ref[...] = norm

    @pl.when(first)
    def _():
        landed(wv_mine, whole_of(wv), wv, sems.at[0])
        landed(im_mine, whole_of(im), im, sems.at[1])

    act, slope = gelu_and_slope(dot(norm, wv[...]))
    act = act.astype(BF16)
    act_ref[...] = act
    slope_ref[...] = slope.astype(BF16)
    drive_ref[...] = dot(act, im[...])
    rows = dead_ref.shape[1]
    width = retain_ref.shape[1]
    retain, inject = spread_rows(retain_ref, rows), spread_rows(inject_ref, rows)

    @pl.when(first)
    def _():
        carry_ref[:rows, :] = jnp.ones((rows, width), F32)
        carry_ref[rows:, :] = jnp.zeros((rows, width), F32)

    def step(t, state):
        through, end = state
        dead = wide(dead_ref[t], width)
        factor = wide(through_ref[t], width) * retain + dead
        return factor * through, factor * end + (1.0 - dead) * inject * drive_ref[at(t, rows), :]

    through, end = lax.fori_loop(
        0, dead_ref.shape[0], step, (carry_ref[:rows, :], carry_ref[rows:, :]), unroll=8
    )
    carry_ref[:rows, :] = through
    carry_ref[rows:, :] = end


def gate_kernel(part, layer, flags, norm_ref, wg_mine, wg_other, act_ref, slope_ref, wg, sems):
    width = wg.shape[1]
    start = pl.multiple_of(flags[2] * (wg_mine.shape[1] // 2) + part * width, LANES)
    window = (pl.ds(0, wg.shape[0]), pl.ds(start, width))

    @pl.when(pl.program_id(0) == 0)
    def _():
        fetch(flags[layer] > 0, wg_mine, wg_other, window, wg, sems.at[0])
        landed(wg_mine, window, wg, sems.at[0])

    act, slope = gelu_and_slope(dot(norm_ref[...], wg[...]))
    act_ref[...] = act.astype(BF16)
    slope_ref[...] = slope.astype(BF16)


def mix_kernel(parts, layer, flags, entry_ref, drive_ref, retain_ref, inject_ref, through_ref, dead_ref, *refs):
    acts, refs = refs[:parts], refs[parts:]
    (
        om_mine, om_other, wm_mine, wm_other, wd_mine, wd_other,
        low_ref, mixer_ref, mix_ref, hidden_ref, branch_ref, om, wm, wd, states, last, sems,
    ) = refs
    first = pl.program_id(0) == 0
    own = flags[layer] > 0
    half = wm.shape[1]
    wm_window = side_window(wm_mine, 1, flags[2], half)
    wd_window = side_window(wd_mine, 0, flags[2], half)

    @pl.when(first)
    def _():
        fetch(own, om_mine, om_other, whole_of(om), om, sems.at[0])
        fetch(own, wm_mine, wm_other, wm_window, wm, sems.at[1])
        fetch(own, wd_mine, wd_other, wd_window, wd, sems.at[2])
        last[...] = entry_ref[...]

    rows = dead_ref.shape[1]
    width = retain_ref.shape[1]
    retain, inject = spread_rows(retain_ref, rows), spread_rows(inject_ref, rows)

    def step(t, state):
        dead = wide(dead_ref[t], width)
        factor = wide(through_ref[t], width) * retain + dead
        state = factor * state + (1.0 - dead) * inject * drive_ref[at(t, rows), :]
        states[at(t, rows), :] = state
        return state

    last[...] = lax.fori_loop(0, dead_ref.shape[0], step, last[...], unroll=8)
    low = states[...].astype(BF16)
    low_ref[...] = low

    @pl.when(first)
    def _():
        landed(om_mine, whole_of(om), om, sems.at[0])
        landed(wm_mine, wm_window, wm, sems.at[1])
        landed(wd_mine, wd_window, wd, sems.at[2])

    mixer = dot(low, om[...]).astype(BF16)
    mixer_ref[...] = mixer
    step_width = half // parts
    branch = None
    for i, act_ref in enumerate(acts):
        here = slice(i * step_width, (i + 1) * step_width)
        value_mix = dot(mixer, wm[:, here])
        mix_ref[:, here] = value_mix.astype(BF16)
        hidden = (act_ref[...].astype(F32) * value_mix).astype(BF16)
        hidden_ref[:, here] = hidden
    branch_ref[...] = dot(hidden_ref[...], wd[...]).astype(BF16)


def middle_kernel(
    parts, layer, flags, entry_ref, drive_ref, grad_ref, retain_ref, inject_ref, through_ref, dead_ref, *refs
):
    acts, slopes, refs = refs[:parts], refs[parts : 2 * parts], refs[2 * parts :]
    (
        om_mine, om_other, wm_mine, wm_other, wd_mine, wd_other,
        low_ref, mixer_ref, hidden_ref, gate_low_ref, mix_low_ref, mixer_back_ref,
        om, wm, wd, states, last, sems,
    ) = refs
    first = pl.program_id(0) == 0
    own = flags[layer] > 0
    half = wm.shape[1]
    wm_window = side_window(wm_mine, 1, flags[2], half)
    wd_window = side_window(wd_mine, 0, flags[2], half)

    @pl.when(first)
    def _():
        fetch(own, om_mine, om_other, whole_of(om), om, sems.at[0])
        fetch(own, wm_mine, wm_other, wm_window, wm, sems.at[1])
        fetch(own, wd_mine, wd_other, wd_window, wd, sems.at[2])
        last[...] = entry_ref[...]

    rows = dead_ref.shape[1]
    width = retain_ref.shape[1]
    retain, inject = spread_rows(retain_ref, rows), spread_rows(inject_ref, rows)

    def step(t, state):
        dead = wide(dead_ref[t], width)
        factor = wide(through_ref[t], width) * retain + dead
        state = factor * state + (1.0 - dead) * inject * drive_ref[at(t, rows), :]
        states[at(t, rows), :] = state
        return state

    last[...] = lax.fori_loop(0, dead_ref.shape[0], step, last[...], unroll=8)
    low = states[...].astype(BF16)
    low_ref[...] = low

    @pl.when(first)
    def _():
        landed(om_mine, whole_of(om), om, sems.at[0])
        landed(wm_mine, wm_window, wm, sems.at[1])
        landed(wd_mine, wd_window, wd, sems.at[2])

    mixer = dot(low, om[...]).astype(BF16)
    mixer_ref[...] = mixer
    step_width = half // parts
    for i in range(parts):
        here = slice(i * step_width, (i + 1) * step_width)
        value_mix = dot(mixer, wm[:, here])
        act = acts[i][...].astype(F32)
        hidden_ref[:, here] = (act * value_mix).astype(BF16)
        d_hidden = dot_t(grad_ref[...], wd[here, :])
        gate_low_ref[:, here] = (slopes[i][...].astype(F32) * (d_hidden * value_mix)).astype(BF16)
        mix_low_ref[:, here] = (d_hidden * act).astype(BF16)
    mixer_back_ref[...] = dot_t(mix_low_ref[...], wm[...]).astype(BF16)


def branch_kernel(layer, flags, hidden_ref, wd_mine, wd_other, branch_ref, wd, sems):
    window = side_window(wd_mine, 0, flags[2], wd.shape[0])

    @pl.when(pl.program_id(0) == 0)
    def _():
        fetch(flags[layer] > 0, wd_mine, wd_other, window, wd, sems.at[0])
        landed(wd_mine, window, wd, sems.at[0])

    branch_ref[...] = dot(hidden_ref[...], wd[...]).astype(BF16)


def hidden_back_kernel(parts, layer, flags, grad_ref, mix_ref, *refs):
    acts, slopes, refs = refs[:parts], refs[parts : 2 * parts], refs[2 * parts :]
    wd_mine, wd_other, wm_mine, wm_other, gate_low_ref, mix_low_ref, mixer_ref, wd, wm, sems = refs
    own = flags[layer] > 0
    half = wm.shape[1]
    wm_window = side_window(wm_mine, 1, flags[2], half)
    wd_window = side_window(wd_mine, 0, flags[2], half)

    @pl.when(pl.program_id(0) == 0)
    def _():
        fetch(own, wd_mine, wd_other, wd_window, wd, sems.at[0])
        fetch(own, wm_mine, wm_other, wm_window, wm, sems.at[1])
        landed(wd_mine, wd_window, wd, sems.at[0])
        landed(wm_mine, wm_window, wm, sems.at[1])

    step_width = half // parts
    for i in range(parts):
        here = slice(i * step_width, (i + 1) * step_width)
        d_hidden = dot_t(grad_ref[...], wd[here, :])
        gate_low_ref[:, here] = (
            slopes[i][...].astype(F32) * (d_hidden * mix_ref[:, here].astype(F32))
        ).astype(BF16)
        mix_low_ref[:, here] = (d_hidden * acts[i][...].astype(F32)).astype(BF16)
    mixer_ref[...] = dot_t(mix_low_ref[...], wm[...]).astype(BF16)


def states_back_kernel(
    layer, flags, mixer_ref, mixer_other, retain_ref, through_ref, dead_ref, om_mine, om_other,
    mixer_low_ref, d_states_ref, carry_ref, om, sems,
):
    first = pl.program_id(0) == 0
    rows = dead_ref.shape[1]
    count = dead_ref.shape[0]
    width = retain_ref.shape[1]

    @pl.when(first)
    def _():
        fetch(flags[layer] > 0, om_mine, om_other, whole_of(om), om, sems.at[0])
        carry_ref[:rows, :] = jnp.ones((rows, width), F32)
        carry_ref[rows:, :] = jnp.zeros((rows, width), F32)
        landed(om_mine, whole_of(om), om, sems.at[0])

    low = (mixer_ref[...].astype(F32) + mixer_other[...].astype(F32)).astype(BF16)
    mixer_low_ref[...] = low
    d_states_ref[...] = dot_t(low, om[...])
    retain = spread_rows(retain_ref, rows)

    def step(i, state):
        t = count - 1 - i
        through, end = state
        factor = wide(through_ref[t], width) * retain + wide(dead_ref[t], width)
        return factor * through, factor * (end + d_states_ref[at(t, rows), :])

    through, end = lax.fori_loop(0, count, step, (carry_ref[:rows, :], carry_ref[rows:, :]), unroll=8)
    carry_ref[:rows, :] = through
    carry_ref[rows:, :] = end


def drive_back_kernel(
    layer, flags, back_ref, entry_ref, d_states_ref, states_ref, drive_ref, retain_ref, inject_ref, gain_ref,
    through_ref, dead_ref, slope_ref, im_mine, im_other,
    drive_low_ref, value_low_ref, rate_ref, im, states, d_drive, kept, sems,
):
    block = pl.program_id(0)
    rows = dead_ref.shape[1]
    count = dead_ref.shape[0]
    width = retain_ref.shape[1]

    @pl.when(block == 0)
    def _():
        fetch(flags[layer] > 0, im_mine, im_other, whole_of(im), im, sems.at[0])
        kept[0] = back_ref[...]
        kept[1] = jnp.zeros((rows, width), F32)
        kept[2] = jnp.zeros((rows, width), F32)
        kept[3] = jnp.zeros((rows, width), F32)
        landed(im_mine, whole_of(im), im, sems.at[0])

    retain, inject = spread_rows(retain_ref, rows), spread_rows(inject_ref, rows)
    states[...] = states_ref[...].astype(F32)

    def step(i, state):
        carried, flow, decay_sum, inject_sum = state
        t = count - 1 - i
        here = at(t, rows)
        dead = wide(dead_ref[t], width)
        lam = d_states_ref[here, :] + carried
        decay_sum = decay_sum + flow * states[here, :]
        alive = (1.0 - dead) * lam
        d_drive[here, :] = alive * inject
        inject_sum = inject_sum + alive * drive_ref[here, :]
        flow = wide(through_ref[t], width) * lam
        return flow * retain + dead * lam, flow, decay_sum, inject_sum

    carried, flow, decay_sum, inject_sum = lax.fori_loop(
        0, count, step, (kept[0], kept[1], kept[2], kept[3]), unroll=8
    )
    kept[0] = carried
    kept[1] = flow
    kept[2] = decay_sum
    kept[3] = inject_sum

    @pl.when(block == pl.num_programs(0) - 1)
    def _():
        rate_ref[...] = jnp.sum(
            gain_ref[...] * inject_sum - retain * (decay_sum + flow * entry_ref[...]), axis=0, keepdims=True
        )

    low = d_drive[...].astype(BF16)
    drive_low_ref[...] = low
    value_low_ref[...] = (slope_ref[...].astype(F32) * dot_t(low, im[...])).astype(BF16)


def gate_back_kernel(layer, flags, gate_low_ref, wg_mine, wg_other, d_norm_ref, wg, sems):
    window = side_window(wg_mine, 1, flags[2], wg.shape[1])

    @pl.when(pl.program_id(0) == 0)
    def _():
        fetch(flags[layer] > 0, wg_mine, wg_other, window, wg, sems.at[0])
        landed(wg_mine, window, wg, sems.at[0])

    d_norm_ref[...] = dot_t(gate_low_ref[...], wg[...]).astype(BF16)


def norm_back_kernel(
    layer, flags, grad_ref, d_norm_ref, d_norm_other, value_low_ref, x_ref, gain_ref, wv_mine, wv_other,
    d_x_ref, d_x_low_ref, vector_ref, wv, sems,
):
    @pl.when(pl.program_id(0) == 0)
    def _():
        fetch(flags[layer] > 0, wv_mine, wv_other, whole_of(wv), wv, sems.at[0])
        vector_ref[...] = jnp.zeros_like(vector_ref)
        landed(wv_mine, whole_of(wv), wv, sems.at[0])

    d_norm = (d_norm_ref[...].astype(F32) + d_norm_other[...].astype(F32)) + dot_t(value_low_ref[...], wv[...])
    centre, rstd = norm_parts(x_ref[...].astype(F32))
    xhat = centre * rstd
    vector_ref[0:1, :] += jnp.sum(d_norm * xhat, axis=0, keepdims=True)
    vector_ref[1:2, :] += jnp.sum(d_norm, axis=0, keepdims=True)
    scaled = d_norm * gain_ref[...]
    first = jnp.mean(scaled, axis=-1, keepdims=True)
    second = jnp.mean(scaled * xhat, axis=-1, keepdims=True)
    d_x = grad_ref[...].astype(F32) + (scaled - first - xhat * second) * rstd
    d_x_ref[...] = d_x
    d_x_low_ref[...] = d_x.astype(BF16)


def shape(dims, dtype):
    return jax.ShapeDtypeStruct(dims, dtype)


def run(kernel, flags, grid, operands, outs, scratch, flops=0, near=()):
    arrays = [far(array) if array.size >= 65536 and id(array) not in near else array for array, _ in operands]
    held = 6 * 1024 * 1024
    for array, spec in operands + outs:
        if spec.block_shape is not None:
            held += 2 * math.prod(spec.block_shape) * array.dtype.itemsize
    for item in scratch:
        if item.dtype in (F32, BF16):
            held += math.prod(item.shape) * item.dtype.itemsize
    return pl.pallas_call(
        kernel,
        out_shape=[struct for struct, _ in outs],
        grid_spec=pltpu.PrefetchScalarGridSpec(
            num_scalar_prefetch=1,
            grid=grid,
            in_specs=[spec for _, spec in operands],
            out_specs=[spec for _, spec in outs],
            scratch_shapes=scratch,
        ),
        cost_estimate=pl.CostEstimate(flops=0, bytes_accessed=0, transcendentals=0),
        compiler_params=pltpu.CompilerParams(
            vmem_limit_bytes=held, dimension_semantics=("arbitrary",) * len(grid)
        ),
    )(flags, *arrays)


def far(array):
    return pltpu.with_memory_space_constraint(array, pltpu.HBM)


def whole(dims):
    return pl.BlockSpec(dims, lambda *_: (0,) * len(dims))


class Reduction:
    def __init__(self, arrays, bits, mine):
        self.left = tuple(sorted(bits, reverse=True))
        self.terms = [(tuple(arrays), self.left, None)]
        self.fixed = {}
        self.mine = mine
        self.height = sum(array.shape[-2] for array in arrays)

    def part(self, fixed):
        left = [bit for bit in self.left if bit not in fixed]
        total = None
        for arrays, bits, at_row in self.terms:
            pieces = []
            for array in arrays:
                block = array.shape[len(bits) :]
                starts = [fixed.get(bit, 0) for bit in bits] + [at_row or 0, 0]
                if at_row is not None:
                    block = (self.height, *block[1:])
                sizes = [1 if bit in fixed else 2 for bit in bits] + list(block)
                pieces.append(lax.dynamic_slice(array, starts, sizes).reshape((2,) * len(left) + tuple(block)))
            term = pieces[0] if len(pieces) == 1 else jnp.concatenate(pieces, axis=-2)
            term = term.astype(F32)
            total = term if total is None else total + term
        return total

    def message(self, bit):
        away = dict(self.fixed)
        away[bit] = 1 - self.mine[bit]
        return self.part(away).astype(BF16)

    def step(self, bit):
        self.send(bit, self.message(bit))

    def send(self, bit, sent):
        count = lax.axis_size("seq")
        self.take(bit, lax.ppermute(sent, "seq", [(i, i ^ (1 << bit)) for i in range(count)]))

    def take(self, bit, came, at_row=0):
        self.fixed[bit] = self.mine[bit]
        self.terms.append(((came,), tuple(b for b in self.left if b not in self.fixed), at_row))

    def result(self):
        return self.part(self.fixed)


def arrived(reductions):
    return [part.terms[-1][0] for part in reductions]


def put_back(reductions, arrays):
    for part, array in zip(reductions, arrays):
        part.terms[-1] = (array, *part.terms[-1][1:])


def awaited(token, *reductions):
    token, came = lax.optimization_barrier((token, arrived(reductions)))
    put_back(reductions, came)
    return token


def carried(pieces, mine, backward, anchor=None, fillers=(), sends=(), waits=()):
    rows = pieces.shape[0] // 2
    count = lax.axis_size("seq")
    through, end = pieces[:rows], pieces[rows:]
    before_through, before_end = jnp.ones_like(through), jnp.zeros_like(end)
    filled = []
    for bit in range(len(mine)):
        message = jnp.concatenate([through, end], axis=0)
        if bit < len(fillers):
            message, anchor, filled = lax.optimization_barrier((message, anchor, filled))
        if bit < len(waits) and waits[bit]:
            message = awaited(message, *waits[bit])
        came = lax.ppermute(message, "seq", [(i, i ^ (1 << bit)) for i in range(count)])
        if bit < len(sends) and sends[bit] is not None:
            sends[bit](filled)
        if bit < len(fillers):
            filled = filled + [fillers[bit](anchor, filled)]
            came, filled = lax.optimization_barrier((came, filled))
        far_through, far_end = came[:rows], came[rows:]
        first = mine[bit] == (0 if backward else 1)
        before_end = jnp.where(first, before_through * far_end + before_end, before_end)
        before_through = jnp.where(first, before_through * far_through, before_through)
        end = jnp.where(first, through * far_end + end, far_through * end + far_end)
        through = through * far_through
    for filler in fillers[len(mine) :]:
        filled = filled + [filler(anchor, filled)]
    return before_through, before_end, filled


def swap(array):
    return lax.ppermute(array, "section", [(0, 1), (1, 0)])


def on_device(
    inputs, cotangent, lengths, keep, init_states, ln_gain, ln_bias, w_gate, w_value, in_map, rates, out_map,
    w_mix, w_down,
):
    rows, count, width = inputs.shape
    tokens = rows * count
    gate_width = w_gate.shape[2]
    half = gate_width // 2
    value_width = w_value.shape[2]
    state_width = in_map.shape[2]
    section = lax.axis_index("section")
    piece = lax.axis_index("seq")
    pieces = lax.axis_size("seq")
    bits = pieces.bit_length() - 1
    mine = [(piece >> bit) & 1 for bit in range(bits)]
    block = 256 if tokens % 256 == 0 else tokens
    grid = (tokens // block,)
    parts = 1

    any_spec = pl.BlockSpec(memory_space=pl.ANY)

    def pair(mine, other):
        return [(far(mine), any_spec), (far(other), any_spec)]

    my_vectors = jnp.concatenate([ln_gain[0], ln_bias[0], rates[0], init_states[0].reshape(-1)])
    vectors = swap(my_vectors)
    wv_other, im_other = swap(w_value[0]), swap(in_map[0])
    wv, im = pair(w_value[0], wv_other), pair(in_map[0], im_other)
    wg_mine, inputs, _, _ = lax.optimization_barrier((w_gate[0], inputs, wv_other, im_other))
    wg = pair(wg_mine, swap(wg_mine))
    flags = jnp.stack([(section == 0).astype(jnp.int32), (section == 1).astype(jnp.int32), section.astype(jnp.int32)])

    grad_top = cotangent.transpose(1, 0, 2).reshape(tokens, width)

    positions = piece * count + jnp.arange(count, dtype=jnp.int32)
    first_len, second_len = lengths[:, 0][None, :], lengths[:, 1][None, :]
    live = positions[:, None] < first_len + second_len
    reset = (positions[:, None] == first_len) & (second_len > 0)
    through = jnp.where(live & jnp.logical_not(reset), keep.T, 0.0)
    dead = jnp.where(live, 0.0, 1.0).astype(F32)
    through = jnp.broadcast_to(through[:, :, None], (count, rows, LANES))
    dead = jnp.broadcast_to(dead[:, :, None], (count, rows, LANES))
    mask_dims = (block // rows, rows, LANES)
    end_block = grid[0] - 1
    mask_spec = pl.BlockSpec(mask_dims, lambda i, f: (i, 0, 0))
    back_mask_spec = pl.BlockSpec(mask_dims, lambda i, f: (end_block - i, 0, 0))
    masks = [(through, mask_spec), (dead, mask_spec)]
    back_masks = [(through, back_mask_spec), (dead, back_mask_spec)]
    near_masks = (id(through), id(dead))

    def by_rows(cols):
        return pl.BlockSpec((block, cols), lambda i, f: (i, 0))

    def by_rows_back(cols):
        return pl.BlockSpec((block, cols), lambda i, f: (end_block - i, 0))

    def out(cols, dtype=BF16, back=False):
        struct = pltpu.HBM((tokens, cols), dtype)
        return (struct, by_rows_back(cols) if back else by_rows(cols))

    def sems(n):
        return pltpu.SemaphoreType.DMA((n,))

    carry_dims = (2 * rows, state_width)
    carry_out = (shape(carry_dims, F32), whole(carry_dims))
    row_state = whole((rows, state_width))
    wv_dims, im_dims, om_dims = (width, value_width), (value_width, state_width), (state_width, value_width)
    wg_dims, wm_dims, wd_dims = (width, half), (value_width, half), (half, width)

    layers = []
    for layer in range(2):
        chosen = jnp.where(section == layer, my_vectors, vectors)
        gain, bias, rate = (
            chosen[:width][None],
            chosen[width : 2 * width][None],
            chosen[2 * width : 2 * width + state_width][None],
        )
        start = chosen[2 * width + state_width :].reshape(rows, state_width)
        inject = jnp.sqrt(-jnp.expm1(-2.0 * rate))
        one_width, one_state = whole((1, width)), whole((1, state_width))
        layers.append(
            dict(
                gain=(gain, one_width),
                bias=(bias, one_width),
                retain=(jnp.exp(-rate), one_state),
                inject=(inject, one_state),
                rate_gain=(jnp.exp(-2.0 * rate) / inject, one_state),
                start=start,
            )
        )

    saved = []
    ends = []
    branch = None
    for layer in range(2):
        now = layers[layer]
        outs = [out(value_width), out(value_width), out(state_width, F32), carry_out]
        if layer == 0:
            by_positions = pl.BlockSpec((rows, block // rows, width), lambda i, f: (0, i, 0))
            norm, x0 = run(
                functools.partial(norm_kernel, layer),
                flags,
                grid,
                [(far(inputs), by_positions), now["gain"], now["bias"]],
                [out(width), out(width)],
                [],
            )
            x = x0
            sources = [(norm, by_rows(width))]
        else:
            sources = [
                (far(x0), by_rows(width)), (far(branch), by_rows(width)), (far(swap(branch)), by_rows(width)),
                now["gain"], now["bias"],
            ]
            outs += [out(width), out(width)]
        value_act, value_slope, drive, pieces_map, *more = run(
            functools.partial(value_kernel, layer),
            flags,
            grid,
            sources + wv + im + [now["retain"], now["inject"]] + masks,
            outs,
            [pltpu.VMEM(wv_dims, BF16), pltpu.VMEM(im_dims, BF16), sems(2)],
            flops=2 * tokens * (width * value_width + value_width * state_width),
            near=near_masks,
        )
        if more:
            x, norm = more
        if layer == 0:
            pieces_map, *rest = lax.optimization_barrier((pieces_map, out_map[0], w_mix[0], w_down[0]))
            om, wm, wd = (pair(array, swap(array)) for array in rest)

        def gate_part(norm, filled, part, layer=layer):
            cols = half // parts
            return run(
                functools.partial(gate_kernel, part, layer),
                flags,
                grid,
                [(norm, by_rows(width))] + wg,
                [out(cols)] * 2,
                [pltpu.VMEM((width, cols), BF16), sems(1)],
                flops=2 * tokens * width * cols,
            )

        before_through, before_end, gates = carried(
            pieces_map, mine, False, norm, [functools.partial(gate_part, part=part) for part in range(parts)]
        )
        gate_act = [act for act, _ in gates]
        gate_slope = [slope for _, slope in gates]
        entry = before_through * now["start"] + before_end
        ends.append(pieces_map[:rows] * entry + pieces_map[rows:])
        if layer == 0:
            states_low, mixer, value_mix, hidden, branch = run(
                functools.partial(mix_kernel, parts, layer),
                flags,
                grid,
                [(entry, row_state), (drive, by_rows(state_width)), now["retain"], now["inject"]]
                + masks
                + [(act, by_rows(half // parts)) for act in gate_act]
                + om
                + wm
                + wd,
                [out(cols) for cols in (state_width, value_width, half, half, width)],
                [
                    pltpu.VMEM(om_dims, BF16),
                    pltpu.VMEM(wm_dims, BF16),
                    pltpu.VMEM(wd_dims, BF16),
                    pltpu.VMEM((block, state_width), F32),
                    pltpu.VMEM((rows, state_width), F32),
                    sems(3),
                ],
                flops=2 * tokens * (state_width * value_width + value_width * half + half * width),
                near=near_masks,
            )
        else:
            value_mix = None
            states_low, mixer, hidden, gate_low, mix_low, mixer_part = run(
                functools.partial(middle_kernel, parts, layer),
                flags,
                grid,
                [
                    (entry, row_state), (drive, by_rows(state_width)), (far(grad_top), by_rows(width)),
                    now["retain"], now["inject"],
                ]
                + masks
                + [(array, by_rows(half // parts)) for array in gate_act + gate_slope]
                + om
                + wm
                + wd,
                [
                    out(state_width), out(value_width), out(half), out(half), out(half),
                    out(value_width),
                ],
                [
                    pltpu.VMEM(om_dims, BF16),
                    pltpu.VMEM(wm_dims, BF16),
                    pltpu.VMEM(wd_dims, BF16),
                    pltpu.VMEM((block, state_width), F32),
                    pltpu.VMEM((rows, state_width), F32),
                    sems(3),
                ],
                flops=2 * tokens * (state_width * value_width + 2 * value_width * half + 2 * half * width),
                near=near_masks,
            )
        saved.append(
            dict(
                x=x, norm=norm, value_act=value_act, value_slope=value_slope, drive=drive, gate_act=gate_act,
                gate_slope=gate_slope, entry=entry, states_low=states_low, mixer=mixer,
                value_mix=value_mix, hidden=hidden,
            )
        )
    x1 = saved[1]["x"]

    def gate_norm_part(layer, gate_low):
        return run(
            functools.partial(gate_back_kernel, layer),
            flags,
            grid,
            [(gate_low, by_rows(half))] + wg,
            [out(width)],
            [pltpu.VMEM(wg_dims, BF16), sems(1)],
            flops=2 * tokens * half * width,
        )[0]

    def hidden_back(layer, grad):
        kept = saved[layer]
        return run(
            functools.partial(hidden_back_kernel, parts, layer),
            flags,
            grid,
            [(grad, by_rows(width)), (far(kept["value_mix"]), by_rows(half))]
            + [(far(array), by_rows(half // parts)) for array in kept["gate_act"] + kept["gate_slope"]]
            + wd
            + wm,
            [out(half), out(half), out(value_width)],
            [pltpu.VMEM(wd_dims, BF16), pltpu.VMEM(wm_dims, BF16), sems(2)],
            flops=2 * tokens * half * (width + value_width),
        )

    def states_back(layer, mixer_part, mixer_other):
        return run(
            functools.partial(states_back_kernel, layer),
            flags,
            grid,
            [
                (far(mixer_part), by_rows_back(value_width)),
                (far(mixer_other), by_rows_back(value_width)),
                layers[layer]["retain"],
            ]
            + back_masks
            + om,
            [
                out(value_width, back=True),
                (shape((tokens, state_width), F32), by_rows_back(state_width)),
                carry_out,
            ],
            [pltpu.VMEM(om_dims, BF16), sems(1)],
            flops=2 * tokens * state_width * value_width,
            near=near_masks,
        )

    def drive_back(layer, back, d_states):
        now, kept = layers[layer], saved[layer]
        return run(
            functools.partial(drive_back_kernel, layer),
            flags,
            grid,
            [
                (back, row_state),
                (kept["entry"], row_state),
                (d_states, by_rows_back(state_width)),
                (far(kept["states_low"]), by_rows_back(state_width)),
                (far(kept["drive"]), by_rows_back(state_width)),
                now["retain"],
                now["inject"],
                now["rate_gain"],
            ]
            + back_masks
            + [(far(kept["value_slope"]), by_rows_back(value_width))]
            + im,
            [
                out(state_width, back=True),
                out(value_width, back=True),
                (shape((1, state_width), F32), whole((1, state_width))),
            ],
            [
                pltpu.VMEM(im_dims, BF16),
                pltpu.VMEM((block, state_width), F32),
                pltpu.VMEM((block, state_width), F32),
                pltpu.VMEM((4, rows, state_width), F32),
                sems(1),
            ],
            flops=2 * tokens * state_width * value_width,
            near=(*near_masks, id(d_states)),
        )

    def norm_back(layer, grad, d_norm_part, d_norm_other, value_low):
        return run(
            functools.partial(norm_back_kernel, layer),
            flags,
            grid,
            [
                (far(grad), by_rows(width)),
                (far(d_norm_part), by_rows(width)),
                (far(d_norm_other), by_rows(width)),
                (value_low, by_rows(value_width)),
                (far(saved[layer]["x"]), by_rows(width)),
                layers[layer]["gain"],
            ]
            + wv,
            [
                out(width, F32),
                out(width),
                (shape((8, width), F32), whole((8, width))),
            ],
            [pltpu.VMEM(wv_dims, BF16), sems(1)],
            flops=2 * tokens * value_width * width,
        )

    def reductions(d_down, d_gate, d_mix):
        return (
            Reduction([d_down.reshape((2,) * (bits - 1) + (-1, width))], range(bits - 1), mine),
            Reduction([d_gate.reshape((2,) * bits + (-1, half))], range(bits), mine),
            Reduction([d_mix.reshape((2,) * bits + (-1, half))], range(bits), mine),
        )

    cols = value_width // 2

    def sides(layer, value_low, drive_low, mixer_low):
        def my_side(array):
            return lax.dynamic_slice(array, (0, section * cols), (tokens, cols))

        return [
            dot_rows(left, my_side(right)).astype(BF16)
            for left, right in (
                (saved[layer]["norm"], value_low),
                (saved[layer]["value_act"], drive_low),
                (saved[layer]["states_low"], mixer_low),
            )
        ]

    def vector_of(norm_vectors, grad_rate):
        vector = jnp.concatenate(
            [
                norm_vectors[0].reshape(pieces, -1),
                norm_vectors[1].reshape(pieces, -1),
                grad_rate.reshape(pieces, -1),
            ],
            axis=1,
        ).astype(BF16)
        return jnp.pad(vector[:, None, :], ((0, 0), (0, 15), (0, cols - vector.shape[1])))

    def small_of(side_grads, *vectors_):
        arrays = [array.reshape(pieces, -1, cols) for array in side_grads] + [vector_of(*v) for v in vectors_]
        (joint,) = tied(jnp.concatenate(arrays, axis=1))
        return joint.reshape((2,) * bits + joint.shape[1:])

    def tied(*arrays):
        return lax.optimization_barrier(arrays)

    def joint_message(reductions, bit):
        return jnp.concatenate([part.message(bit) for part in reductions], axis=-2)

    def joint_send(reductions, bit, message):
        came = lax.ppermute(message, "seq", [(i, i ^ (1 << bit)) for i in range(pieces)])
        at_row = 0
        for part in reductions:
            part.take(bit, came, at_row)
            at_row += part.height

    def joint_step(reductions, bit):
        joint_send(reductions, bit, joint_message(reductions, bit))

    def final_down(layer, part):
        top = pieces // 2
        sent = part.astype(BF16)
        mate = 1 - layer
        across = [
            pair
            for low in range(top)
            for pair in (
                (layer * pieces + mate * top + low, layer * pieces + layer * top + low),
                (mate * pieces + layer * top + low, layer * pieces + mate * top + low),
            )
        ]
        beside = [(mate * pieces + mate * top + low, layer * pieces + mate * top + low) for low in range(top)]
        came = lax.ppermute(sent, ("section", "seq"), across).astype(F32)
        came = came + lax.ppermute(sent, ("section", "seq"), beside).astype(F32)
        return jnp.where(mine[bits - 1] == layer, part, 0.0) + came

    share = value_width // pieces
    order = list(range(bits - 1))
    down_order = order
    gate_order = order[1:2] + order[:1] + order[2:]
    mix_order = order[-1:] + order[:-1]
    small_order = [*mix_order[:1], *order[1:-1], *order[:1], bits - 1] if len(order) > 1 else [*order, bits - 1]
    orders = (down_order, gate_order, mix_order)

    def back_carry(layer, back_map, d_down, grads, with_norm):
        parts_ = [Reduction([d_down.reshape((2,) * (bits - 1) + (-1, width))], range(bits - 1), mine)]

        def gate_filler(a, filled):
            return dot_rows(a[0], a[1]).astype(BF16), parts_[0].message(down_order[0])

        def norm_filler(a, filled):
            gate = Reduction([filled[0][0].reshape((2,) * bits + (-1, half))], range(bits), mine)
            parts_.append(gate)
            message = gate.message(gate_order[0])
            return (message, gate_norm_part(layer, a[1])) if with_norm else (message,)

        def mix_filler(a, filled):
            mix = Reduction(
                [dot_rows(a[2], a[3]).astype(BF16).reshape((2,) * bits + (-1, half))], range(bits), mine
            )
            parts_.append(mix)
            return mix.message(mix_order[0])

        sends = [
            None,
            lambda filled: parts_[0].send(down_order[0], filled[0][1]),
            lambda filled: parts_[1].send(gate_order[0], filled[1][0]),
        ]
        _, back, filled = carried(back_map, mine, True, grads, [gate_filler, norm_filler, mix_filler], sends)
        back, message = tied(back, filled[2])
        parts_[2].send(mix_order[0], message)
        return back, parts_, filled[1][-1]

    kept = saved[1]
    mixer_other = swap(mixer_part)
    d_down = dot_rows(kept["hidden"], grad_top).astype(BF16)
    mixer_low, d_states, back_map = states_back(1, mixer_part, mixer_other)
    back_map, d_down = tied(back_map, d_down)
    back, ones, d_norm_part = back_carry(
        1, back_map, d_down, (kept["norm"], gate_low, kept["mixer"], mix_low), True
    )
    down_one, gate_one, mix_one = ones
    d_norm_other = swap(d_norm_part)
    drive_low, value_low, grad_rate = drive_back(1, back, d_states)
    value_low = awaited(value_low, down_one)
    value_low, message = tied(value_low, down_one.message(down_order[1]))
    down_one.send(down_order[1], message)
    d_x1, grad, norm_vectors = norm_back(1, grad_top, d_norm_part, d_norm_other, value_low)
    small_one = small_of(sides(1, value_low, drive_low, mixer_low), (norm_vectors, grad_rate))
    grad, small_one = awaited((grad, small_one), gate_one, mix_one)
    grad, small_one, message = tied(grad, small_one, joint_message(ones[1:], order[0]))
    small_one = Reduction([small_one], range(bits), mine)
    joint_send(ones[1:], order[0], message)
    small_one.step(small_order[0])

    kept = saved[0]
    gate_low, mix_low, mixer_part = hidden_back(0, grad)
    mixer_other = swap(mixer_part)
    d_norm_part = gate_norm_part(0, gate_low)
    grad, mix_low, gate_low, d_norm_part = awaited(
        (grad, mix_low, gate_low, d_norm_part), down_one, gate_one, mix_one, small_one
    )
    d_norm_other = swap(d_norm_part)
    for place in range(2, len(order)):
        for part, order_ in zip(ones, orders):
            part.step(order_[place])
    d_down = dot_rows(kept["hidden"], grad).astype(BF16)
    mixer_part, mixer_other, d_down, d_norm_other = tied(mixer_part, mixer_other, d_down, d_norm_other)
    mixer_low, d_states, back_map = states_back(0, mixer_part, mixer_other)
    back_map, d_down = awaited((back_map, d_down), *ones)
    back, zeros, _ = back_carry(0, back_map, d_down, (kept["norm"], gate_low, kept["mixer"], mix_low), False)
    down_zero, gate_zero, mix_zero = zeros
    drive_low, value_low, grad_rate = drive_back(0, back, d_states)
    d_x0, _, norm_vectors = norm_back(0, grad, d_norm_part, d_norm_other, value_low)
    token = awaited((norm_vectors, value_low, drive_low), down_zero, gate_zero, mix_zero)
    joint_step(zeros[1:], order[0])
    down_zero.step(down_order[1])
    joint_step(ones[1:], bits - 1)
    grad_down_one = final_down(1, down_one.result())
    norm_vectors, value_low, drive_low = token
    small_zero = Reduction([small_of(sides(0, value_low, drive_low, mixer_low))], range(bits), mine)
    small_zero.step(small_order[0])
    hidden_one, _ = tied(saved[1]["hidden"], norm_vectors)
    (branch,) = run(
        functools.partial(branch_kernel, 1),
        flags,
        grid,
        [(hidden_one, by_rows(half))] + wd,
        [out(width)],
        [pltpu.VMEM(wd_dims, BF16), sems(1)],
    )
    branch = awaited(branch, down_zero)
    for place in range(2, len(order)):
        down_zero.step(down_order[place])
    (token, branch, x1, d_x0, d_x1, grad_down_one) = awaited(
        (norm_vectors, branch, x1, d_x0, d_x1, grad_down_one), *zeros[1:], *ones[1:], small_zero
    )
    for place in range(2, len(order)):
        for part, order_ in zip(zeros[1:], orders[1:]):
            part.step(order_[place])
    smalls = (small_one, small_zero)
    joint_step(smalls, small_order[-2])
    vector_zero = vector_of(token, grad_rate)
    vector_zero = Reduction([vector_zero.reshape((2,) * bits + vector_zero.shape[1:])], range(bits), mine)
    vector_zero.step(1)
    branch_other = swap(branch)
    token = awaited(token, *zeros, *smalls, vector_zero)
    message = joint_message(zeros[1:], bits - 1)
    joint_send(zeros[1:], bits - 1, message)
    last, _ = tied(arrived((*smalls, vector_zero, down_zero)), message)
    put_back((*smalls, vector_zero, down_zero), last)
    for place in range(1, len(order) - 1):
        joint_step(smalls, small_order[place])
    grad_down_zero = final_down(0, down_zero.result())
    for bit in (0, *range(2, bits - 1)):
        vector_zero.step(bit)
    second_out = (x1.astype(F32) + (branch.astype(F32) + branch_other.astype(F32))).astype(BF16)

    def by_row(array):
        return array.reshape(count, rows, width).transpose(1, 0, 2)[None]

    block_out = by_row(jnp.where(section == 0, x1, second_out))
    token, block_out = awaited((token, block_out), *smalls, vector_zero, *zeros[1:])
    joint_step((*smalls, vector_zero), bits - 1)
    reduced = [
        [grad_down_zero, gate_zero.result(), mix_zero.result()],
        [grad_down_one, gate_one.result(), mix_one.result(), small_one.result()],
    ]
    reduced[0].append(jnp.concatenate([small_zero.result(), vector_zero.result()], axis=0))
    d_xs = [d_x0, d_x1]

    keep_own = [jnp.where(section == 0, a, b) for a, b in zip(reduced[0], reduced[1])]
    give = [jnp.where(section == 0, b, a).astype(BF16) for a, b in zip(reduced[0][1:], reduced[1][1:])]
    taken_wide = swap(jnp.concatenate(give[:2], axis=0))
    taken_small = swap(give[2]).astype(F32)
    cut = give[0].shape[0]
    taken = [taken_wide[:cut].astype(F32), taken_wide[cut:].astype(F32)]

    def joined(own, other):
        return jnp.where(
            section == 0, jnp.concatenate([own, other], axis=-1), jnp.concatenate([other, own], axis=-1)
        )

    grad_down = keep_own[0]
    grad_gate = joined(keep_own[1], taken[0])
    grad_mix = joined(keep_own[2], taken[1])
    small = joined(keep_own[3], taken_small)
    part = width // pieces
    grad_value, grad_input, grad_output = small[:part], small[part : part + share], small[part + share : part + 2 * share]
    vector = keep_own[3][part + 2 * share]
    grad_gain, grad_bias = vector[:part], vector[part : 2 * part]
    grad_rates = vector[2 * part : 2 * part + state_width // pieces]
    grad_in = jnp.where(section == 0, d_xs[0], d_xs[1])
    end_states = jnp.where(section == 0, ends[0], ends[1])

    return (
        block_out,
        by_row(grad_in),
        end_states[None, :, None, :],
        grad_gain[None],
        grad_bias[None],
        grad_gate[None],
        grad_value[None],
        grad_input[None],
        grad_rates[None],
        grad_output[None],
        grad_mix[None],
        grad_down[None],
    )


def solution(mesh):
    in_specs = (
        P(None, "seq", None),
        P(None, "seq", None),
        P(),
        P(None, "seq"),
        P("section", None, None),
        P("section", None),
        P("section", None),
        P("section", None, None),
        P("section", None, None),
        P("section", None, None),
        P("section", None),
        P("section", None, None),
        P("section", None, None),
        P("section", None, None),
    )
    out_specs = (
        P("section", None, "seq", None),
        P("section", None, "seq", None),
        P("section", None, "seq", None),
        P("section", "seq"),
        P("section", "seq"),
        P("section", "seq", None),
        P("section", "seq", None),
        P("section", "seq", None),
        P("section", "seq"),
        P("section", "seq", None),
        P("section", "seq", None),
        P("section", "seq", None),
    )
    return jax.shard_map(on_device, mesh=mesh, in_specs=in_specs, out_specs=out_specs, check_vma=False)
```

```python
import functools
import math

import jax
import jax.numpy as jnp
from jax import lax
from jax.experimental import pallas as pl
from jax.experimental.pallas import tpu as pltpu
from jax.sharding import PartitionSpec as P

F32 = jnp.float32
BF16 = jnp.bfloat16
VMEM_BYTES = 56 * 1024 * 1024
LANES = 128


def gelu_and_slope(v):
    half_sq = jnp.exp(-0.5 * v * v)
    t = 1.0 / (1.0 + (0.3275911 * 0.7071067811865476) * jnp.abs(v))
    poly = t * (
        0.127414796 + t * (-0.142248368 + t * (0.7107068705 + t * (-0.7265760135 + t * 0.5307027145)))
    )
    tail = poly * half_sq
    cdf = jnp.where(v >= 0.0, 1.0 - tail, tail)
    return v * cdf, cdf + v * half_sq * 0.3989422804014327


def dot(left, right):
    return jnp.dot(left, right, preferred_element_type=F32)


def dot_t(left, right):
    return lax.dot_general(left, right, (((1,), (1,)), ((), ())), preferred_element_type=F32)


def dot_rows(left, right):
    return lax.dot_general(left, right, (((0,), (0,)), ((), ())), preferred_element_type=F32)


def fetch(own, mine, other, window, kept, sem):
    @pl.when(own)
    def _():
        pltpu.make_async_copy(mine.at[window], kept, sem).start()

    @pl.when(jnp.logical_not(own))
    def _():
        pltpu.make_async_copy(other.at[window], kept, sem).start()


def landed(mine, window, kept, sem):
    pltpu.make_async_copy(mine.at[window], kept, sem).wait()


def whole_of(ref):
    return tuple(pl.ds(0, size) for size in ref.shape)


def side_window(ref, axis, side, width):
    start = pl.multiple_of(side * width, LANES)
    return tuple(pl.ds(start, width) if d == axis else pl.ds(0, size) for d, size in enumerate(ref.shape))


def wide(values, width):
    return jnp.concatenate([values] * (width // LANES), axis=1)


def norm_parts(x):
    centre = x - jnp.mean(x, axis=-1, keepdims=True)
    spread = jnp.mean(centre * centre, axis=-1, keepdims=True)
    return centre, lax.rsqrt(spread + 1e-05)


def normed(x, gain_ref, bias_ref):
    centre, rstd = norm_parts(x)
    return (centre * rstd * gain_ref[...] + bias_ref[...]).astype(BF16)


def spread_rows(ref, rows):
    return jnp.broadcast_to(ref[...], (rows, ref.shape[1]))


def at(t, rows):
    return pl.ds(pl.multiple_of(t * rows, rows), rows)


def norm_kernel(layer, flags, x_ref, gain_ref, bias_ref, norm_ref, turned_ref):
    x = jnp.swapaxes(x_ref[...].astype(F32), 0, 1).reshape(norm_ref.shape)
    turned_ref[...] = x.astype(BF16)
    norm_ref[...] = normed(x, gain_ref, bias_ref)


def value_kernel(layer, flags, *refs):
    if layer == 0:
        norm_ref, *refs = refs
    else:
        x_ref, y_ref, z_ref, gain_ref, bias_ref, *refs = refs
    (wv_mine, wv_other, im_mine, im_other, retain_ref, inject_ref, through_ref, dead_ref, *refs) = refs
    if layer == 0:
        act_ref, slope_ref, drive_ref, carry_ref, wv, im, sems = refs
    else:
        act_ref, slope_ref, drive_ref, carry_ref, x1_ref, norm_ref, wv, im, sems = refs
    first = pl.program_id(0) == 0
    own = flags[layer] > 0

    @pl.when(first)
    def _():
        fetch(own, wv_mine, wv_other, whole_of(wv), wv, sems.at[0])
        fetch(own, im_mine, im_other, whole_of(im), im, sems.at[1])

    if layer == 0:
        norm = norm_ref[...]
    else:
        low = (x_ref[...].astype(F32) + (y_ref[...].astype(F32) + z_ref[...].astype(F32))).astype(BF16)
        x1_ref[...] = low
        norm = normed(low.astype(F32), gain_ref, bias_ref)
        norm_ref[...] = norm

    @pl.when(first)
    def _():
        landed(wv_mine, whole_of(wv), wv, sems.at[0])
        landed(im_mine, whole_of(im), im, sems.at[1])

    act, slope = gelu_and_slope(dot(norm, wv[...]))
    act = act.astype(BF16)
    act_ref[...] = act
    slope_ref[...] = slope.astype(BF16)
    drive_ref[...] = dot(act, im[...])
    rows = dead_ref.shape[1]
    width = retain_ref.shape[1]
    retain, inject = spread_rows(retain_ref, rows), spread_rows(inject_ref, rows)

    @pl.when(first)
    def _():
        carry_ref[:rows, :] = jnp.ones((rows, width), F32)
        carry_ref[rows:, :] = jnp.zeros((rows, width), F32)

    def step(t, state):
        through, end = state
        dead = wide(dead_ref[t], width)
        factor = wide(through_ref[t], width) * retain + dead
        return factor * through, factor * end + (1.0 - dead) * inject * drive_ref[at(t, rows), :]

    through, end = lax.fori_loop(
        0, dead_ref.shape[0], step, (carry_ref[:rows, :], carry_ref[rows:, :]), unroll=8
    )
    carry_ref[:rows, :] = through
    carry_ref[rows:, :] = end


def gate_kernel(part, layer, flags, norm_ref, wg_mine, wg_other, act_ref, slope_ref, wg, sems):
    width = wg.shape[1]
    start = pl.multiple_of(flags[2] * (wg_mine.shape[1] // 2) + part * width, LANES)
    window = (pl.ds(0, wg.shape[0]), pl.ds(start, width))

    @pl.when(pl.program_id(0) == 0)
    def _():
        fetch(flags[layer] > 0, wg_mine, wg_other, window, wg, sems.at[0])
        landed(wg_mine, window, wg, sems.at[0])

    act, slope = gelu_and_slope(dot(norm_ref[...], wg[...]))
    act_ref[...] = act.astype(BF16)
    slope_ref[...] = slope.astype(BF16)


def mix_kernel(parts, layer, flags, entry_ref, drive_ref, retain_ref, inject_ref, through_ref, dead_ref, *refs):
    acts, refs = refs[:parts], refs[parts:]
    (
        om_mine, om_other, wm_mine, wm_other, wd_mine, wd_other,
        low_ref, mixer_ref, mix_ref, hidden_ref, branch_ref, om, wm, wd, states, last, sems,
    ) = refs
    first = pl.program_id(0) == 0
    own = flags[layer] > 0
    half = wm.shape[1]
    wm_window = side_window(wm_mine, 1, flags[2], half)
    wd_window = side_window(wd_mine, 0, flags[2], half)

    @pl.when(first)
    def _():
        fetch(own, om_mine, om_other, whole_of(om), om, sems.at[0])
        fetch(own, wm_mine, wm_other, wm_window, wm, sems.at[1])
        fetch(own, wd_mine, wd_other, wd_window, wd, sems.at[2])
        last[...] = entry_ref[...]

    rows = dead_ref.shape[1]
    width = retain_ref.shape[1]
    retain, inject = spread_rows(retain_ref, rows), spread_rows(inject_ref, rows)

    def step(t, state):
        dead = wide(dead_ref[t], width)
        factor = wide(through_ref[t], width) * retain + dead
        state = factor * state + (1.0 - dead) * inject * drive_ref[at(t, rows), :]
        states[at(t, rows), :] = state
        return state

    last[...] = lax.fori_loop(0, dead_ref.shape[0], step, last[...], unroll=8)
    low = states[...].astype(BF16)
    low_ref[...] = low

    @pl.when(first)
    def _():
        landed(om_mine, whole_of(om), om, sems.at[0])
        landed(wm_mine, wm_window, wm, sems.at[1])
        landed(wd_mine, wd_window, wd, sems.at[2])

    mixer = dot(low, om[...]).astype(BF16)
    mixer_ref[...] = mixer
    step_width = half // parts
    branch = None
    for i, act_ref in enumerate(acts):
        here = slice(i * step_width, (i + 1) * step_width)
        value_mix = dot(mixer, wm[:, here])
        mix_ref[:, here] = value_mix.astype(BF16)
        hidden = (act_ref[...].astype(F32) * value_mix).astype(BF16)
        hidden_ref[:, here] = hidden
    branch_ref[...] = dot(hidden_ref[...], wd[...]).astype(BF16)


def middle_kernel(
    parts, layer, flags, entry_ref, drive_ref, grad_ref, retain_ref, inject_ref, through_ref, dead_ref, *refs
):
    acts, slopes, refs = refs[:parts], refs[parts : 2 * parts], refs[2 * parts :]
    (
        om_mine, om_other, wm_mine, wm_other, wd_mine, wd_other,
        low_ref, mixer_ref, hidden_ref, gate_low_ref, mix_low_ref, mixer_back_ref,
        om, wm, wd, states, last, sems,
    ) = refs
    first = pl.program_id(0) == 0
    own = flags[layer] > 0
    half = wm.shape[1]
    wm_window = side_window(wm_mine, 1, flags[2], half)
    wd_window = side_window(wd_mine, 0, flags[2], half)

    @pl.when(first)
    def _():
        fetch(own, om_mine, om_other, whole_of(om), om, sems.at[0])
        fetch(own, wm_mine, wm_other, wm_window, wm, sems.at[1])
        fetch(own, wd_mine, wd_other, wd_window, wd, sems.at[2])
        last[...] = entry_ref[...]

    rows = dead_ref.shape[1]
    width = retain_ref.shape[1]
    retain, inject = spread_rows(retain_ref, rows), spread_rows(inject_ref, rows)

    def step(t, state):
        dead = wide(dead_ref[t], width)
        factor = wide(through_ref[t], width) * retain + dead
        state = factor * state + (1.0 - dead) * inject * drive_ref[at(t, rows), :]
        states[at(t, rows), :] = state
        return state

    last[...] = lax.fori_loop(0, dead_ref.shape[0], step, last[...], unroll=8)
    low = states[...].astype(BF16)
    low_ref[...] = low

    @pl.when(first)
    def _():
        landed(om_mine, whole_of(om), om, sems.at[0])
        landed(wm_mine, wm_window, wm, sems.at[1])
        landed(wd_mine, wd_window, wd, sems.at[2])

    mixer = dot(low, om[...]).astype(BF16)
    mixer_ref[...] = mixer
    step_width = half // parts
    for i in range(parts):
        here = slice(i * step_width, (i + 1) * step_width)
        value_mix = dot(mixer, wm[:, here])
        act = acts[i][...].astype(F32)
        hidden_ref[:, here] = (act * value_mix).astype(BF16)
        d_hidden = dot_t(grad_ref[...], wd[here, :])
        gate_low_ref[:, here] = (slopes[i][...].astype(F32) * (d_hidden * value_mix)).astype(BF16)
        mix_low_ref[:, here] = (d_hidden * act).astype(BF16)
    mixer_back_ref[...] = dot_t(mix_low_ref[...], wm[...]).astype(BF16)


def branch_kernel(layer, flags, hidden_ref, wd_mine, wd_other, branch_ref, wd, sems):
    window = side_window(wd_mine, 0, flags[2], wd.shape[0])

    @pl.when(pl.program_id(0) == 0)
    def _():
        fetch(flags[layer] > 0, wd_mine, wd_other, window, wd, sems.at[0])
        landed(wd_mine, window, wd, sems.at[0])

    branch_ref[...] = dot(hidden_ref[...], wd[...]).astype(BF16)


def hidden_back_kernel(parts, layer, flags, grad_ref, mix_ref, *refs):
    acts, slopes, refs = refs[:parts], refs[parts : 2 * parts], refs[2 * parts :]
    wd_mine, wd_other, wm_mine, wm_other, gate_low_ref, mix_low_ref, mixer_ref, wd, wm, sems = refs
    own = flags[layer] > 0
    half = wm.shape[1]
    wm_window = side_window(wm_mine, 1, flags[2], half)
    wd_window = side_window(wd_mine, 0, flags[2], half)

    @pl.when(pl.program_id(0) == 0)
    def _():
        fetch(own, wd_mine, wd_other, wd_window, wd, sems.at[0])
        fetch(own, wm_mine, wm_other, wm_window, wm, sems.at[1])
        landed(wd_mine, wd_window, wd, sems.at[0])
        landed(wm_mine, wm_window, wm, sems.at[1])

    step_width = half // parts
    for i in range(parts):
        here = slice(i * step_width, (i + 1) * step_width)
        d_hidden = dot_t(grad_ref[...], wd[here, :])
        gate_low_ref[:, here] = (
            slopes[i][...].astype(F32) * (d_hidden * mix_ref[:, here].astype(F32))
        ).astype(BF16)
        mix_low_ref[:, here] = (d_hidden * acts[i][...].astype(F32)).astype(BF16)
    mixer_ref[...] = dot_t(mix_low_ref[...], wm[...]).astype(BF16)


def states_back_kernel(
    layer, flags, mixer_ref, mixer_other, retain_ref, through_ref, dead_ref, om_mine, om_other,
    mixer_low_ref, d_states_ref, carry_ref, om, sems,
):
    first = pl.program_id(0) == 0
    rows = dead_ref.shape[1]
    count = dead_ref.shape[0]
    width = retain_ref.shape[1]

    @pl.when(first)
    def _():
        fetch(flags[layer] > 0, om_mine, om_other, whole_of(om), om, sems.at[0])
        carry_ref[:rows, :] = jnp.ones((rows, width), F32)
        carry_ref[rows:, :] = jnp.zeros((rows, width), F32)
        landed(om_mine, whole_of(om), om, sems.at[0])

    low = (mixer_ref[...].astype(F32) + mixer_other[...].astype(F32)).astype(BF16)
    mixer_low_ref[...] = low
    d_states_ref[...] = dot_t(low, om[...])
    retain = spread_rows(retain_ref, rows)

    def step(i, state):
        t = count - 1 - i
        through, end = state
        factor = wide(through_ref[t], width) * retain + wide(dead_ref[t], width)
        return factor * through, factor * (end + d_states_ref[at(t, rows), :])

    through, end = lax.fori_loop(0, count, step, (carry_ref[:rows, :], carry_ref[rows:, :]), unroll=8)
    carry_ref[:rows, :] = through
    carry_ref[rows:, :] = end


def drive_back_kernel(
    layer, flags, back_ref, entry_ref, d_states_ref, states_ref, drive_ref, retain_ref, inject_ref, gain_ref,
    through_ref, dead_ref, slope_ref, im_mine, im_other,
    drive_low_ref, value_low_ref, rate_ref, im, states, d_drive, kept, sems,
):
    block = pl.program_id(0)
    rows = dead_ref.shape[1]
    count = dead_ref.shape[0]
    width = retain_ref.shape[1]

    @pl.when(block == 0)
    def _():
        fetch(flags[layer] > 0, im_mine, im_other, whole_of(im), im, sems.at[0])
        kept[0] = back_ref[...]
        kept[1] = jnp.zeros((rows, width), F32)
        kept[2] = jnp.zeros((rows, width), F32)
        kept[3] = jnp.zeros((rows, width), F32)
        landed(im_mine, whole_of(im), im, sems.at[0])

    retain, inject = spread_rows(retain_ref, rows), spread_rows(inject_ref, rows)
    states[...] = states_ref[...].astype(F32)

    def step(i, state):
        carried, flow, decay_sum, inject_sum = state
        t = count - 1 - i
        here = at(t, rows)
        dead = wide(dead_ref[t], width)
        lam = d_states_ref[here, :] + carried
        decay_sum = decay_sum + flow * states[here, :]
        alive = (1.0 - dead) * lam
        d_drive[here, :] = alive * inject
        inject_sum = inject_sum + alive * drive_ref[here, :]
        flow = wide(through_ref[t], width) * lam
        return flow * retain + dead * lam, flow, decay_sum, inject_sum

    carried, flow, decay_sum, inject_sum = lax.fori_loop(
        0, count, step, (kept[0], kept[1], kept[2], kept[3]), unroll=8
    )
    kept[0] = carried
    kept[1] = flow
    kept[2] = decay_sum
    kept[3] = inject_sum

    @pl.when(block == pl.num_programs(0) - 1)
    def _():
        rate_ref[...] = jnp.sum(
            gain_ref[...] * inject_sum - retain * (decay_sum + flow * entry_ref[...]), axis=0, keepdims=True
        )

    low = d_drive[...].astype(BF16)
    drive_low_ref[...] = low
    value_low_ref[...] = (slope_ref[...].astype(F32) * dot_t(low, im[...])).astype(BF16)


def gate_back_kernel(layer, flags, gate_low_ref, wg_mine, wg_other, d_norm_ref, wg, sems):
    window = side_window(wg_mine, 1, flags[2], wg.shape[1])

    @pl.when(pl.program_id(0) == 0)
    def _():
        fetch(flags[layer] > 0, wg_mine, wg_other, window, wg, sems.at[0])
        landed(wg_mine, window, wg, sems.at[0])

    d_norm_ref[...] = dot_t(gate_low_ref[...], wg[...]).astype(BF16)


def norm_back_kernel(
    layer, flags, grad_ref, d_norm_ref, d_norm_other, value_low_ref, x_ref, gain_ref, wv_mine, wv_other,
    d_x_ref, d_x_low_ref, vector_ref, wv, sems,
):
    @pl.when(pl.program_id(0) == 0)
    def _():
        fetch(flags[layer] > 0, wv_mine, wv_other, whole_of(wv), wv, sems.at[0])
        vector_ref[...] = jnp.zeros_like(vector_ref)
        landed(wv_mine, whole_of(wv), wv, sems.at[0])

    d_norm = (d_norm_ref[...].astype(F32) + d_norm_other[...].astype(F32)) + dot_t(value_low_ref[...], wv[...])
    centre, rstd = norm_parts(x_ref[...].astype(F32))
    xhat = centre * rstd
    vector_ref[0:1, :] += jnp.sum(d_norm * xhat, axis=0, keepdims=True)
    vector_ref[1:2, :] += jnp.sum(d_norm, axis=0, keepdims=True)
    scaled = d_norm * gain_ref[...]
    first = jnp.mean(scaled, axis=-1, keepdims=True)
    second = jnp.mean(scaled * xhat, axis=-1, keepdims=True)
    d_x = grad_ref[...].astype(F32) + (scaled - first - xhat * second) * rstd
    d_x_ref[...] = d_x
    d_x_low_ref[...] = d_x.astype(BF16)


def shape(dims, dtype):
    return jax.ShapeDtypeStruct(dims, dtype)


def run(kernel, flags, grid, operands, outs, scratch, flops=0, near=()):
    arrays = [far(array) if array.size >= 65536 and id(array) not in near else array for array, _ in operands]
    held = 6 * 1024 * 1024
    for array, spec in operands + outs:
        if spec.block_shape is not None:
            held += 2 * math.prod(spec.block_shape) * array.dtype.itemsize
    for item in scratch:
        if item.dtype in (F32, BF16):
            held += math.prod(item.shape) * item.dtype.itemsize
    return pl.pallas_call(
        kernel,
        out_shape=[struct for struct, _ in outs],
        grid_spec=pltpu.PrefetchScalarGridSpec(
            num_scalar_prefetch=1,
            grid=grid,
            in_specs=[spec for _, spec in operands],
            out_specs=[spec for _, spec in outs],
            scratch_shapes=scratch,
        ),
        cost_estimate=pl.CostEstimate(flops=0, bytes_accessed=0, transcendentals=0),
        compiler_params=pltpu.CompilerParams(
            vmem_limit_bytes=held, dimension_semantics=("arbitrary",) * len(grid)
        ),
    )(flags, *arrays)


def far(array):
    return pltpu.with_memory_space_constraint(array, pltpu.HBM)


def whole(dims):
    return pl.BlockSpec(dims, lambda *_: (0,) * len(dims))


class Reduction:
    def __init__(self, arrays, bits, mine):
        self.left = tuple(sorted(bits, reverse=True))
        self.terms = [(tuple(arrays), self.left, None)]
        self.fixed = {}
        self.mine = mine
        self.height = sum(array.shape[-2] for array in arrays)

    def part(self, fixed):
        left = [bit for bit in self.left if bit not in fixed]
        total = None
        for arrays, bits, at_row in self.terms:
            pieces = []
            for array in arrays:
                block = array.shape[len(bits) :]
                starts = [fixed.get(bit, 0) for bit in bits] + [at_row or 0, 0]
                if at_row is not None:
                    block = (self.height, *block[1:])
                sizes = [1 if bit in fixed else 2 for bit in bits] + list(block)
                pieces.append(lax.dynamic_slice(array, starts, sizes).reshape((2,) * len(left) + tuple(block)))
            term = pieces[0] if len(pieces) == 1 else jnp.concatenate(pieces, axis=-2)
            term = term.astype(F32)
            total = term if total is None else total + term
        return total

    def message(self, bit):
        away = dict(self.fixed)
        away[bit] = 1 - self.mine[bit]
        return self.part(away).astype(BF16)

    def step(self, bit):
        self.send(bit, self.message(bit))

    def send(self, bit, sent):
        count = lax.axis_size("seq")
        self.take(bit, lax.ppermute(sent, "seq", [(i, i ^ (1 << bit)) for i in range(count)]))

    def take(self, bit, came, at_row=0):
        self.fixed[bit] = self.mine[bit]
        self.terms.append(((came,), tuple(b for b in self.left if b not in self.fixed), at_row))

    def result(self):
        return self.part(self.fixed)


def arrived(reductions):
    return [part.terms[-1][0] for part in reductions]


def put_back(reductions, arrays):
    for part, array in zip(reductions, arrays):
        part.terms[-1] = (array, *part.terms[-1][1:])


def awaited(token, *reductions):
    token, came = lax.optimization_barrier((token, arrived(reductions)))
    put_back(reductions, came)
    return token


def carried(pieces, mine, backward, anchor=None, fillers=(), sends=(), waits=()):
    rows = pieces.shape[0] // 2
    count = lax.axis_size("seq")
    through, end = pieces[:rows], pieces[rows:]
    before_through, before_end = jnp.ones_like(through), jnp.zeros_like(end)
    filled = []
    for bit in range(len(mine)):
        message = jnp.concatenate([through, end], axis=0)
        if bit < len(fillers):
            message, anchor, filled = lax.optimization_barrier((message, anchor, filled))
        if bit < len(waits) and waits[bit]:
            message = awaited(message, *waits[bit])
        came = lax.ppermute(message, "seq", [(i, i ^ (1 << bit)) for i in range(count)])
        if bit < len(sends) and sends[bit] is not None:
            sends[bit](filled)
        if bit < len(fillers):
            filled = filled + [fillers[bit](anchor, filled)]
            came, filled = lax.optimization_barrier((came, filled))
        far_through, far_end = came[:rows], came[rows:]
        first = mine[bit] == (0 if backward else 1)
        before_end = jnp.where(first, before_through * far_end + before_end, before_end)
        before_through = jnp.where(first, before_through * far_through, before_through)
        end = jnp.where(first, through * far_end + end, far_through * end + far_end)
        through = through * far_through
    for filler in fillers[len(mine) :]:
        filled = filled + [filler(anchor, filled)]
    return before_through, before_end, filled


def swap(array):
    return lax.ppermute(array, "section", [(0, 1), (1, 0)])


def on_device(
    inputs, cotangent, lengths, keep, init_states, ln_gain, ln_bias, w_gate, w_value, in_map, rates, out_map,
    w_mix, w_down,
):
    rows, count, width = inputs.shape
    tokens = rows * count
    gate_width = w_gate.shape[2]
    half = gate_width // 2
    value_width = w_value.shape[2]
    state_width = in_map.shape[2]
    section = lax.axis_index("section")
    piece = lax.axis_index("seq")
    pieces = lax.axis_size("seq")
    bits = pieces.bit_length() - 1
    mine = [(piece >> bit) & 1 for bit in range(bits)]
    block = 256 if tokens % 256 == 0 else tokens
    grid = (tokens // block,)
    parts = 1

    any_spec = pl.BlockSpec(memory_space=pl.ANY)

    def pair(mine, other):
        return [(far(mine), any_spec), (far(other), any_spec)]

    my_vectors = jnp.concatenate([ln_gain[0], ln_bias[0], rates[0], init_states[0].reshape(-1)])
    vectors = swap(my_vectors)
    wv_other, im_other = swap(w_value[0]), swap(in_map[0])
    wv, im = pair(w_value[0], wv_other), pair(in_map[0], im_other)
    wg_mine, inputs, _, _ = lax.optimization_barrier((w_gate[0], inputs, wv_other, im_other))
    wg = pair(wg_mine, swap(wg_mine))
    flags = jnp.stack([(section == 0).astype(jnp.int32), (section == 1).astype(jnp.int32), section.astype(jnp.int32)])

    grad_top = cotangent.transpose(1, 0, 2).reshape(tokens, width)

    positions = piece * count + jnp.arange(count, dtype=jnp.int32)
    first_len, second_len = lengths[:, 0][None, :], lengths[:, 1][None, :]
    live = positions[:, None] < first_len + second_len
    reset = (positions[:, None] == first_len) & (second_len > 0)
    through = jnp.where(live & jnp.logical_not(reset), keep.T, 0.0)
    dead = jnp.where(live, 0.0, 1.0).astype(F32)
    through = jnp.broadcast_to(through[:, :, None], (count, rows, LANES))
    dead = jnp.broadcast_to(dead[:, :, None], (count, rows, LANES))
    mask_dims = (block // rows, rows, LANES)
    end_block = grid[0] - 1
    mask_spec = pl.BlockSpec(mask_dims, lambda i, f: (i, 0, 0))
    back_mask_spec = pl.BlockSpec(mask_dims, lambda i, f: (end_block - i, 0, 0))
    masks = [(through, mask_spec), (dead, mask_spec)]
    back_masks = [(through, back_mask_spec), (dead, back_mask_spec)]
    near_masks = (id(through), id(dead))

    def by_rows(cols):
        return pl.BlockSpec((block, cols), lambda i, f: (i, 0))

    def by_rows_back(cols):
        return pl.BlockSpec((block, cols), lambda i, f: (end_block - i, 0))

    def out(cols, dtype=BF16, back=False):
        struct = pltpu.HBM((tokens, cols), dtype)
        return (struct, by_rows_back(cols) if back else by_rows(cols))

    def sems(n):
        return pltpu.SemaphoreType.DMA((n,))

    carry_dims = (2 * rows, state_width)
    carry_out = (shape(carry_dims, F32), whole(carry_dims))
    row_state = whole((rows, state_width))
    wv_dims, im_dims, om_dims = (width, value_width), (value_width, state_width), (state_width, value_width)
    wg_dims, wm_dims, wd_dims = (width, half), (value_width, half), (half, width)

    layers = []
    for layer in range(2):
        chosen = jnp.where(section == layer, my_vectors, vectors)
        gain, bias, rate = (
            chosen[:width][None],
            chosen[width : 2 * width][None],
            chosen[2 * width : 2 * width + state_width][None],
        )
        start = chosen[2 * width + state_width :].reshape(rows, state_width)
        inject = jnp.sqrt(-jnp.expm1(-2.0 * rate))
        one_width, one_state = whole((1, width)), whole((1, state_width))
        layers.append(
            dict(
                gain=(gain, one_width),
                bias=(bias, one_width),
                retain=(jnp.exp(-rate), one_state),
                inject=(inject, one_state),
                rate_gain=(jnp.exp(-2.0 * rate) / inject, one_state),
                start=start,
            )
        )

    saved = []
    ends = []
    branch = None
    for layer in range(2):
        now = layers[layer]
        outs = [out(value_width), out(value_width), out(state_width, F32), carry_out]
        if layer == 0:
            by_positions = pl.BlockSpec((rows, block // rows, width), lambda i, f: (0, i, 0))
            norm, x0 = run(
                functools.partial(norm_kernel, layer),
                flags,
                grid,
                [(far(inputs), by_positions), now["gain"], now["bias"]],
                [out(width), out(width)],
                [],
            )
            x = x0
            sources = [(norm, by_rows(width))]
        else:
            sources = [
                (far(x0), by_rows(width)), (far(branch), by_rows(width)), (far(swap(branch)), by_rows(width)),
                now["gain"], now["bias"],
            ]
            outs += [out(width), out(width)]
        value_act, value_slope, drive, pieces_map, *more = run(
            functools.partial(value_kernel, layer),
            flags,
            grid,
            sources + wv + im + [now["retain"], now["inject"]] + masks,
            outs,
            [pltpu.VMEM(wv_dims, BF16), pltpu.VMEM(im_dims, BF16), sems(2)],
            flops=2 * tokens * (width * value_width + value_width * state_width),
            near=near_masks,
        )
        if more:
            x, norm = more
        if layer == 0:
            pieces_map, *rest = lax.optimization_barrier((pieces_map, out_map[0], w_mix[0], w_down[0]))
            om, wm, wd = (pair(array, swap(array)) for array in rest)

        def gate_part(norm, filled, part, layer=layer):
            cols = half // parts
            return run(
                functools.partial(gate_kernel, part, layer),
                flags,
                grid,
                [(norm, by_rows(width))] + wg,
                [out(cols)] * 2,
                [pltpu.VMEM((width, cols), BF16), sems(1)],
                flops=2 * tokens * width * cols,
            )

        before_through, before_end, gates = carried(
            pieces_map, mine, False, norm, [functools.partial(gate_part, part=part) for part in range(parts)]
        )
        gate_act = [act for act, _ in gates]
        gate_slope = [slope for _, slope in gates]
        entry = before_through * now["start"] + before_end
        ends.append(pieces_map[:rows] * entry + pieces_map[rows:])
        if layer == 0:
            states_low, mixer, value_mix, hidden, branch = run(
                functools.partial(mix_kernel, parts, layer),
                flags,
                grid,
                [(entry, row_state), (drive, by_rows(state_width)), now["retain"], now["inject"]]
                + masks
                + [(act, by_rows(half // parts)) for act in gate_act]
                + om
                + wm
                + wd,
                [out(cols) for cols in (state_width, value_width, half, half, width)],
                [
                    pltpu.VMEM(om_dims, BF16),
                    pltpu.VMEM(wm_dims, BF16),
                    pltpu.VMEM(wd_dims, BF16),
                    pltpu.VMEM((block, state_width), F32),
                    pltpu.VMEM((rows, state_width), F32),
                    sems(3),
                ],
                flops=2 * tokens * (state_width * value_width + value_width * half + half * width),
                near=near_masks,
            )
        else:
            value_mix = None
            states_low, mixer, hidden, gate_low, mix_low, mixer_part = run(
                functools.partial(middle_kernel, parts, layer),
                flags,
                grid,
                [
                    (entry, row_state), (drive, by_rows(state_width)), (far(grad_top), by_rows(width)),
                    now["retain"], now["inject"],
                ]
                + masks
                + [(array, by_rows(half // parts)) for array in gate_act + gate_slope]
                + om
                + wm
                + wd,
                [
                    out(state_width), out(value_width), out(half), out(half), out(half),
                    out(value_width),
                ],
                [
                    pltpu.VMEM(om_dims, BF16),
                    pltpu.VMEM(wm_dims, BF16),
                    pltpu.VMEM(wd_dims, BF16),
                    pltpu.VMEM((block, state_width), F32),
                    pltpu.VMEM((rows, state_width), F32),
                    sems(3),
                ],
                flops=2 * tokens * (state_width * value_width + 2 * value_width * half + 2 * half * width),
                near=near_masks,
            )
        saved.append(
            dict(
                x=x, norm=norm, value_act=value_act, value_slope=value_slope, drive=drive, gate_act=gate_act,
                gate_slope=gate_slope, entry=entry, states_low=states_low, mixer=mixer,
                value_mix=value_mix, hidden=hidden,
            )
        )
    x1 = saved[1]["x"]

    def gate_norm_part(layer, gate_low):
        return run(
            functools.partial(gate_back_kernel, layer),
            flags,
            grid,
            [(gate_low, by_rows(half))] + wg,
            [out(width)],
            [pltpu.VMEM(wg_dims, BF16), sems(1)],
            flops=2 * tokens * half * width,
        )[0]

    def hidden_back(layer, grad):
        kept = saved[layer]
        return run(
            functools.partial(hidden_back_kernel, parts, layer),
            flags,
            grid,
            [(grad, by_rows(width)), (far(kept["value_mix"]), by_rows(half))]
            + [(far(array), by_rows(half // parts)) for array in kept["gate_act"] + kept["gate_slope"]]
            + wd
            + wm,
            [out(half), out(half), out(value_width)],
            [pltpu.VMEM(wd_dims, BF16), pltpu.VMEM(wm_dims, BF16), sems(2)],
            flops=2 * tokens * half * (width + value_width),
        )

    def states_back(layer, mixer_part, mixer_other):
        return run(
            functools.partial(states_back_kernel, layer),
            flags,
            grid,
            [
                (far(mixer_part), by_rows_back(value_width)),
                (far(mixer_other), by_rows_back(value_width)),
                layers[layer]["retain"],
            ]
            + back_masks
            + om,
            [
                out(value_width, back=True),
                (shape((tokens, state_width), F32), by_rows_back(state_width)),
                carry_out,
            ],
            [pltpu.VMEM(om_dims, BF16), sems(1)],
            flops=2 * tokens * state_width * value_width,
            near=near_masks,
        )

    def drive_back(layer, back, d_states):
        now, kept = layers[layer], saved[layer]
        return run(
            functools.partial(drive_back_kernel, layer),
            flags,
            grid,
            [
                (back, row_state),
                (kept["entry"], row_state),
                (d_states, by_rows_back(state_width)),
                (far(kept["states_low"]), by_rows_back(state_width)),
                (far(kept["drive"]), by_rows_back(state_width)),
                now["retain"],
                now["inject"],
                now["rate_gain"],
            ]
            + back_masks
            + [(far(kept["value_slope"]), by_rows_back(value_width))]
            + im,
            [
                out(state_width, back=True),
                out(value_width, back=True),
                (shape((1, state_width), F32), whole((1, state_width))),
            ],
            [
                pltpu.VMEM(im_dims, BF16),
                pltpu.VMEM((block, state_width), F32),
                pltpu.VMEM((block, state_width), F32),
                pltpu.VMEM((4, rows, state_width), F32),
                sems(1),
            ],
            flops=2 * tokens * state_width * value_width,
            near=(*near_masks, id(d_states)),
        )

    def norm_back(layer, grad, d_norm_part, d_norm_other, value_low):
        return run(
            functools.partial(norm_back_kernel, layer),
            flags,
            grid,
            [
                (far(grad), by_rows(width)),
                (far(d_norm_part), by_rows(width)),
                (far(d_norm_other), by_rows(width)),
                (value_low, by_rows(value_width)),
                (far(saved[layer]["x"]), by_rows(width)),
                layers[layer]["gain"],
            ]
            + wv,
            [
                out(width, F32),
                out(width),
                (shape((8, width), F32), whole((8, width))),
            ],
            [pltpu.VMEM(wv_dims, BF16), sems(1)],
            flops=2 * tokens * value_width * width,
        )

    def reductions(d_down, d_gate, d_mix):
        return (
            Reduction([d_down.reshape((2,) * (bits - 1) + (-1, width))], range(bits - 1), mine),
            Reduction([d_gate.reshape((2,) * bits + (-1, half))], range(bits), mine),
            Reduction([d_mix.reshape((2,) * bits + (-1, half))], range(bits), mine),
        )

    cols = value_width // 2

    def sides(layer, value_low, drive_low, mixer_low):
        def my_side(array):
            return lax.dynamic_slice(array, (0, section * cols), (tokens, cols))

        return [
            dot_rows(left, my_side(right)).astype(BF16)
            for left, right in (
                (saved[layer]["norm"], value_low),
                (saved[layer]["value_act"], drive_low),
                (saved[layer]["states_low"], mixer_low),
            )
        ]

    def vector_of(norm_vectors, grad_rate):
        vector = jnp.concatenate(
            [
                norm_vectors[0].reshape(pieces, -1),
                norm_vectors[1].reshape(pieces, -1),
                grad_rate.reshape(pieces, -1),
            ],
            axis=1,
        ).astype(BF16)
        return jnp.pad(vector[:, None, :], ((0, 0), (0, 15), (0, cols - vector.shape[1])))

    def small_of(side_grads, *vectors_):
        arrays = [array.reshape(pieces, -1, cols) for array in side_grads] + [vector_of(*v) for v in vectors_]
        (joint,) = tied(jnp.concatenate(arrays, axis=1))
        return joint.reshape((2,) * bits + joint.shape[1:])

    def tied(*arrays):
        return lax.optimization_barrier(arrays)

    def joint_message(reductions, bit):
        return jnp.concatenate([part.message(bit) for part in reductions], axis=-2)

    def joint_send(reductions, bit, message):
        came = lax.ppermute(message, "seq", [(i, i ^ (1 << bit)) for i in range(pieces)])
        at_row = 0
        for part in reductions:
            part.take(bit, came, at_row)
            at_row += part.height

    def joint_step(reductions, bit):
        joint_send(reductions, bit, joint_message(reductions, bit))

    def final_down(layer, part):
        top = pieces // 2
        sent = part.astype(BF16)
        mate = 1 - layer
        across = [
            pair
            for low in range(top)
            for pair in (
                (layer * pieces + mate * top + low, layer * pieces + layer * top + low),
                (mate * pieces + layer * top + low, layer * pieces + mate * top + low),
            )
        ]
        beside = [(mate * pieces + mate * top + low, layer * pieces + mate * top + low) for low in range(top)]
        return part, lax.ppermute(sent, ("section", "seq"), across), lax.ppermute(sent, ("section", "seq"), beside)

    def down_sum(layer, part, far_part, near_part):
        own = jnp.where(mine[bits - 1] == layer, part, 0.0)
        return own + (far_part.astype(F32) + near_part.astype(F32))

    share = value_width // pieces
    order = list(range(bits - 1))
    down_order = order
    gate_order = order[1:2] + order[:1] + order[2:]
    mix_order = order[-1:] + order[:-1]
    small_order = [*mix_order[:1], *order[1:-1], *order[:1], bits - 1] if len(order) > 1 else [*order, bits - 1]
    orders = (down_order, gate_order, mix_order)

    def back_carry(layer, back_map, d_down, grads, with_norm):
        parts_ = [Reduction([d_down.reshape((2,) * (bits - 1) + (-1, width))], range(bits - 1), mine)]

        def gate_filler(a, filled):
            return dot_rows(a[0], a[1]).astype(BF16), parts_[0].message(down_order[0])

        def norm_filler(a, filled):
            gate = Reduction([filled[0][0].reshape((2,) * bits + (-1, half))], range(bits), mine)
            parts_.append(gate)
            message = gate.message(gate_order[0])
            return (message, gate_norm_part(layer, a[1])) if with_norm else (message,)

        def mix_filler(a, filled):
            mix = Reduction(
                [dot_rows(a[2], a[3]).astype(BF16).reshape((2,) * bits + (-1, half))], range(bits), mine
            )
            parts_.append(mix)
            return mix.message(mix_order[0])

        sends = [
            None,
            lambda filled: parts_[0].send(down_order[0], filled[0][1]),
            lambda filled: parts_[1].send(gate_order[0], filled[1][0]),
        ]
        _, back, filled = carried(back_map, mine, True, grads, [gate_filler, norm_filler, mix_filler], sends)
        back, message = tied(back, filled[2])
        parts_[2].send(mix_order[0], message)
        return back, parts_, filled[1][-1]

    kept = saved[1]
    mixer_other = swap(mixer_part)
    d_down = dot_rows(kept["hidden"], grad_top).astype(BF16)
    mixer_low, d_states, back_map = states_back(1, mixer_part, mixer_other)
    back_map, d_down = tied(back_map, d_down)
    back, ones, d_norm_part = back_carry(
        1, back_map, d_down, (kept["norm"], gate_low, kept["mixer"], mix_low), True
    )
    down_one, gate_one, mix_one = ones
    d_norm_other = swap(d_norm_part)
    drive_low, value_low, grad_rate = drive_back(1, back, d_states)
    value_low = awaited(value_low, down_one)
    value_low, message = tied(value_low, down_one.message(down_order[1]))
    down_one.send(down_order[1], message)
    d_x1, grad, norm_vectors = norm_back(1, grad_top, d_norm_part, d_norm_other, value_low)
    small_one = small_of(sides(1, value_low, drive_low, mixer_low), (norm_vectors, grad_rate))
    grad, small_one = awaited((grad, small_one), gate_one, mix_one)
    grad, small_one, message = tied(grad, small_one, joint_message(ones[1:], order[0]))
    small_one = Reduction([small_one], range(bits), mine)
    joint_send(ones[1:], order[0], message)
    small_one.step(small_order[0])

    kept = saved[0]
    gate_low, mix_low, mixer_part = hidden_back(0, grad)
    mixer_other = swap(mixer_part)
    d_norm_part = gate_norm_part(0, gate_low)
    grad, mix_low, gate_low, d_norm_part = awaited(
        (grad, mix_low, gate_low, d_norm_part), down_one, gate_one, mix_one, small_one
    )
    d_norm_other = swap(d_norm_part)
    for place in range(2, len(order)):
        for part, order_ in zip(ones, orders):
            part.step(order_[place])
    d_down = dot_rows(kept["hidden"], grad).astype(BF16)
    mixer_part, mixer_other, d_down, d_norm_other = tied(mixer_part, mixer_other, d_down, d_norm_other)
    mixer_low, d_states, back_map = states_back(0, mixer_part, mixer_other)
    back_map, d_down = awaited((back_map, d_down), *ones)
    back, zeros, _ = back_carry(0, back_map, d_down, (kept["norm"], gate_low, kept["mixer"], mix_low), False)
    down_zero, gate_zero, mix_zero = zeros
    drive_low, value_low, grad_rate = drive_back(0, back, d_states)
    d_x0, _, norm_vectors = norm_back(0, grad, d_norm_part, d_norm_other, value_low)
    token = awaited((norm_vectors, value_low, drive_low), down_zero, gate_zero, mix_zero)
    joint_step(zeros[1:], order[0])
    down_zero.step(down_order[1])
    joint_step(ones[1:], bits - 1)
    grad_down_one = down_sum(1, *final_down(1, down_one.result()))
    norm_vectors, value_low, drive_low = token
    small_zero = Reduction([small_of(sides(0, value_low, drive_low, mixer_low))], range(bits), mine)
    small_zero.step(small_order[0])
    hidden_one, _ = tied(saved[1]["hidden"], norm_vectors)
    (branch,) = run(
        functools.partial(branch_kernel, 1),
        flags,
        grid,
        [(hidden_one, by_rows(half))] + wd,
        [out(width)],
        [pltpu.VMEM(wd_dims, BF16), sems(1)],
    )
    branch = awaited(branch, down_zero)
    for place in range(2, len(order)):
        down_zero.step(down_order[place])
    (token, branch, x1, d_x0, d_x1, grad_down_one) = awaited(
        (norm_vectors, branch, x1, d_x0, d_x1, grad_down_one), *zeros[1:], *ones[1:], small_zero
    )
    for place in range(2, len(order)):
        for part, order_ in zip(zeros[1:], orders[1:]):
            part.step(order_[place])
    smalls = (small_one, small_zero)
    joint_step(smalls, small_order[-2])
    vector_zero = vector_of(token, grad_rate)
    vector_zero = Reduction([vector_zero.reshape((2,) * bits + vector_zero.shape[1:])], range(bits), mine)
    vector_zero.step(1)
    branch_other = swap(branch)
    token = awaited(token, *zeros, *smalls, vector_zero)
    message = joint_message(zeros[1:], bits - 1)
    joint_send(zeros[1:], bits - 1, message)
    last, _ = tied(arrived((*smalls, vector_zero, down_zero)), message)
    put_back((*smalls, vector_zero, down_zero), last)
    for place in range(1, len(order) - 1):
        joint_step(smalls, small_order[place])
    down_last = final_down(0, down_zero.result())
    for bit in (0, *range(2, bits - 1)):
        vector_zero.step(bit)
    second_out = (x1.astype(F32) + (branch.astype(F32) + branch_other.astype(F32))).astype(BF16)

    def by_row(array):
        return array.reshape(count, rows, width).transpose(1, 0, 2)[None]

    block_out = by_row(jnp.where(section == 0, x1, second_out))
    token, block_out = awaited((token, block_out), *smalls, vector_zero, *zeros[1:])
    joint_step((*smalls, vector_zero), bits - 1)
    token, down_last = tied(token, down_last)
    grad_down_zero = down_sum(0, *down_last)
    reduced = [
        [grad_down_zero, gate_zero.result(), mix_zero.result()],
        [grad_down_one, gate_one.result(), mix_one.result(), small_one.result()],
    ]
    reduced[0].append(jnp.concatenate([small_zero.result(), vector_zero.result()], axis=0))
    d_xs = [d_x0, d_x1]

    keep_own = [jnp.where(section == 0, a, b) for a, b in zip(reduced[0], reduced[1])]
    give = [jnp.where(section == 0, b, a).astype(BF16) for a, b in zip(reduced[0][1:], reduced[1][1:])]
    taken_wide = swap(jnp.concatenate(give[:2], axis=0))
    taken_small = swap(give[2]).astype(F32)
    cut = give[0].shape[0]
    taken = [taken_wide[:cut].astype(F32), taken_wide[cut:].astype(F32)]

    def joined(own, other):
        return jnp.where(
            section == 0, jnp.concatenate([own, other], axis=-1), jnp.concatenate([other, own], axis=-1)
        )

    grad_down = keep_own[0]
    grad_gate = joined(keep_own[1], taken[0])
    grad_mix = joined(keep_own[2], taken[1])
    small = joined(keep_own[3], taken_small)
    part = width // pieces
    grad_value, grad_input, grad_output = small[:part], small[part : part + share], small[part + share : part + 2 * share]
    vector = keep_own[3][part + 2 * share]
    grad_gain, grad_bias = vector[:part], vector[part : 2 * part]
    grad_rates = vector[2 * part : 2 * part + state_width // pieces]
    grad_in = jnp.where(section == 0, d_xs[0], d_xs[1])
    end_states = jnp.where(section == 0, ends[0], ends[1])

    return (
        block_out,
        by_row(grad_in),
        end_states[None, :, None, :],
        grad_gain[None],
        grad_bias[None],
        grad_gate[None],
        grad_value[None],
        grad_input[None],
        grad_rates[None],
        grad_output[None],
        grad_mix[None],
        grad_down[None],
    )


def solution(mesh):
    in_specs = (
        P(None, "seq", None),
        P(None, "seq", None),
        P(),
        P(None, "seq"),
        P("section", None, None),
        P("section", None),
        P("section", None),
        P("section", None, None),
        P("section", None, None),
        P("section", None, None),
        P("section", None),
        P("section", None, None),
        P("section", None, None),
        P("section", None, None),
    )
    out_specs = (
        P("section", None, "seq", None),
        P("section", None, "seq", None),
        P("section", None, "seq", None),
        P("section", "seq"),
        P("section", "seq"),
        P("section", "seq", None),
        P("section", "seq", None),
        P("section", "seq", None),
        P("section", "seq"),
        P("section", "seq", None),
        P("section", "seq", None),
        P("section", "seq", None),
    )
    return jax.shard_map(on_device, mesh=mesh, in_specs=in_specs, out_specs=out_specs, check_vma=False)
```
